512 devices in a mesh: replica: 32 (over z, x), tensor: 16 (over y, core).
Axes of the slice: x: 4, y: 8, z: 8, core: 2. Of those that a mesh axis runs over, the one named last changes fastest.
Arguments:
- queries: bfloat16 [4, 128, 8192], P(None, 'replica'), may hold values from -16 to 16
- new_entries: bfloat16 [4, 128, 8, 256], P(None, 'replica'), may hold values from -6 to 6
- cache: bfloat16 [128, 8, 512, 256], P('replica', None, 'tensor'), may hold values from -6 to 6
- lengths: int32 [128], P('replica'), may hold values from 2 to 512
- adapter_pages: bfloat16 [256, 2, 64, 8192], P('replica', None, None, 'tensor'), may hold values from -0.75 to 0.75
- request_slots: int32 [128], P('replica'), may hold values from 0 to 39
- source_replica: int32 [1024, 1], P('replica'), may hold values from 0 to 31; in each aligned block of 32 rows (0 to 31, 32 to 63, ...) at most 2 rows name the same one
- source_slot: int32 [1024], P('replica'), may hold values from 0 to 7
Outputs:
- attended: bfloat16 [4, 128, 8192], P(None, 'replica', 'tensor')
- adapted: bfloat16 [4, 128, 8192], P(None, 'replica', 'tensor')
The draws below stay inside these ranges and needn't reach their ends.
Inputs may be any that keep to these rules, and one draw needn't show every extreme that they name: `source_replica`: within the 32 plan entries of one replica no source replica appears more than 2 times, and some replica's plan names one source exactly 2 times.
All inputs are finite; a program needn't handle non-finite values.
Results may differ from the reference program's by a relative error of at most 0.019.
Values may be sent and summed in bfloat16 or wider, within the bound.
No kernel may reach another device: no remote copies, remote signals or barrier semaphores. Data moves between devices by JAX's collectives and lax.ppermute only.
A program may use at most 128 MiB of HBM per device.

```python
import math
import jax
import jax.numpy as jnp
import numpy as np
from jax import lax

D = 8192
HEADS = 64
KV_HEADS = 8
HEAD_DIM = 128
RANK = 64
STEPS = 4
CAP = 2
ROWS = 4
CACHE = 512
SLOTS = 8
MIGRATE = 32
ROWS_TOTAL = 128
PAGES_TOTAL = 256
MOVES_TOTAL = 1024
N_REPLICA = 32


def draw_cache(key, part):
    key = jax.random.fold_in(key, 3)
    shape = (ROWS_TOTAL, KV_HEADS, CACHE, 2 * HEAD_DIM)
    whole = jnp.clip(jax.random.normal(key, shape, jnp.float32), -6.0, 6.0)
    return whole.astype(jnp.bfloat16)


def draw_queries(key, part):
    key = jax.random.fold_in(key, 5)
    broad_key = jax.random.fold_in(key, 7)
    shape = (STEPS, ROWS_TOTAL, D)
    whole = jnp.clip(jax.random.normal(key, shape, jnp.float32), -6.0, 6.0)
    row_ids = jnp.arange(ROWS_TOTAL)
    broad = jax.random.uniform(broad_key, shape, jnp.float32, -16.0, 16.0)
    whole = jnp.where((row_ids % 4 == 1)[None, :, None], broad, whole)
    return whole.astype(jnp.bfloat16)


def touch_ends(array, rng, smallest, high):
    shape = array.shape
    spot = [jax.random.randint(jax.random.fold_in(rng, axis), (), 0, shape[axis]) for axis in range(len(shape))]
    array = array.at[tuple(spot)].set(smallest)
    longest = shape.index(max(shape))
    spot[longest] = (spot[longest] + 1) % shape[longest]
    return array.at[tuple(spot)].set(high)


def block_scale(stream_key, dims, cuts, low, high):
    loudness, own = 1.0, jax.random.fold_in(stream_key, 6)
    for axis_at, blocks in cuts:
        heights = jnp.exp(jax.random.uniform(jax.random.fold_in(own, axis_at), (blocks,), jnp.float32, low / len(cuts), high / len(cuts)))
        loudness = loudness * jnp.repeat(heights, dims[axis_at] // blocks).reshape([-1 if axis == axis_at else 1 for axis in range(len(dims))])
    return loudness


def rank_table(count, skew):
    portions = [(1 << 20) // math.isqrt(rank ** skew) + 1 for rank in range(1, count + 1)]
    width = 1 + sum(portions) // (1 << 30)
    return np.cumsum(np.array([max(1, weight // width) for weight in portions]))


def ranked(rng, extent, amount, slope):
    grid = rank_table(amount, slope)
    pick = jax.random.randint(jax.random.fold_in(rng, 1), extent, 0, int(grid[amount - 1]))
    standing = jnp.searchsorted(jnp.asarray(grid, jnp.int32), pick, side="right")
    return jax.random.permutation(jax.random.fold_in(rng, 2), amount)[standing].astype(jnp.int32)


def assign_block(stream_key, own, number, rows, count, top, reach, skew):
    ranking = jax.random.permutation(stream_key, count)
    crowded, common = portions_of(count, rows * top, reach, skew, True), portions_of(count, rows * top, reach, skew, False)
    places = jnp.arange(count)

    def named(sizes, rotation):
        used = int((sizes > 0).sum())
        fixed = max(1, used // 4)
        moved = fixed + (places - fixed + rotation * (used - fixed)) % max(1, count - fixed)
        return jnp.zeros((count,), jnp.int32).at[ranking[jnp.where(places < fixed, places, moved)]].set(jnp.asarray(sizes, jnp.int32))

    sizes = jnp.where(number % 4 == 0, named(crowded, number // 4), named(common, number - number // 4 - 1))
    mixed = jax.random.permutation(jax.random.fold_in(own, 3), count)
    source_of, receiver = mixed[0:count // 2 * 2:2], mixed[1:count // 2 * 2:2]
    slack = jnp.minimum(sizes[source_of] - 1, reach - sizes[receiver]) // 2
    slack = jnp.where((source_of == ranking[0]) | (receiver == ranking[0]) | (sizes[receiver] == 0), 0, jnp.maximum(slack, 0))
    moved = jax.random.randint(jax.random.fold_in(own, 4), (count // 2,), 0, 1 << 20) % (slack + 1)
    sizes = sizes.at[source_of].add(-moved).at[receiver].add(moved)
    labels = jnp.searchsorted(jnp.cumsum(sizes), jnp.arange(rows * top), side="right").astype(jnp.int32)
    listing = labels.reshape(top, rows).T
    listing = listing[jax.random.permutation(jax.random.fold_in(own, 1), rows)]
    rotation = jax.random.randint(jax.random.fold_in(own, 2), (rows, 1), 0, top)
    return jnp.take_along_axis(listing, (jnp.arange(top)[None, :] + rotation) % top, axis=1)


def portions_of(number_of, total, limit, lean, full):
    weights = [(1 << 20) // math.isqrt(rank ** lean) + 1 for rank in range(1, number_of + 1)]
    largest = limit if full else min(limit, max(-(-total // number_of), total * weights[0] // sum(weights)))
    least = 1 if total - largest >= number_of - 1 else 0
    given, rest = [largest] + [least] * (number_of - 1), total - largest - least * (number_of - 1)
    while rest > 0:
        candidates = [i for i in range(1, number_of) if given[i] < largest] or [i for i in range(1, number_of) if given[i] < limit]
        pool, left = sum([weights[i] for i in candidates]), rest
        for i in candidates:
            addition = min(limit - given[i], max(1, left * weights[i] // pool), rest)
            given[i] = given[i] + addition
            rest = rest - addition
    return np.array(given)


def centred(own_key, extent, spread, limit, shards=(), kind=jnp.bfloat16):
    drawn = spread * jax.random.normal(own_key, extent, jnp.float32)
    if shards:
        drawn = drawn * block_scale(own_key, extent, shards, -0.22, 0.18)
    return jnp.clip(drawn, -limit, limit).astype(kind)


def setup_inputs(seed: int = 0) -> dict:
    streams_of = jax.random.split(jax.random.key(seed), 9)
    queries = draw_queries(jax.random.fold_in(streams_of[8], 71), 0)
    new_entries = centred(streams_of[1], (STEPS, ROWS_TOTAL, KV_HEADS, 2 * HEAD_DIM), 1.0, 6.0, ((1, 32),))
    cache = draw_cache(jax.random.fold_in(streams_of[8], 71), 0)
    lengths = touch_ends(jax.random.randint(streams_of[3], (ROWS_TOTAL,), 2, CACHE + 1), jax.random.fold_in(streams_of[3], 1), 2, CACHE).astype(jnp.int32)
    adapter_pages = centred(streams_of[4], (PAGES_TOTAL, 2, RANK, D), 0.125, 0.75, ((0, 32), (3, 16)))
    request_slots = touch_ends(ranked(streams_of[5], (ROWS_TOTAL,), SLOTS + MIGRATE, 2), jax.random.fold_in(streams_of[5], 3), 0, (SLOTS + MIGRATE) - 1).astype(jnp.int32)
    source_replica_keys = jax.random.split(jax.random.fold_in(streams_of[6], 1), MOVES_TOTAL // MIGRATE)
    source_replica_turns = jax.random.permutation(jax.random.fold_in(streams_of[6], 3), MOVES_TOTAL // MIGRATE)
    source_replica = jax.vmap(lambda own, number: assign_block(jax.random.fold_in(streams_of[6], 2), own, number, MIGRATE, N_REPLICA, 1, CAP, 0))(source_replica_keys, source_replica_turns).reshape((MOVES_TOTAL, 1))
    source_slot = touch_ends(jax.random.randint(streams_of[7], (MOVES_TOTAL,), 0, SLOTS), jax.random.fold_in(streams_of[7], 1), 0, SLOTS - 1).astype(jnp.int32)
    return {"queries": queries, "new_entries": new_entries, "cache": cache, "lengths": lengths, "adapter_pages": adapter_pages, "request_slots": request_slots, "source_replica": source_replica, "source_slot": source_slot}


neg_large = -1.0e30
adapter_scale = 0.5


def page_table(request_slots, source_replica, source_slot):
    row_ids = jnp.arange(ROWS_TOTAL, dtype=jnp.int32)
    owner = row_ids // ROWS
    incoming = jnp.clip(request_slots - SLOTS, 0, MIGRATE - 1)
    entry = owner * MIGRATE + incoming
    remote = source_replica[entry, 0] * SLOTS + source_slot[entry]
    return jnp.where(request_slots < SLOTS, owner * SLOTS + request_slots, remote).astype(jnp.int32)


def reference(queries, new_entries, cache, lengths, adapter_pages, request_slots, source_replica, source_slot):
    page_index = page_table(request_slots, source_replica, source_slot)
    query_group_width = HEADS // KV_HEADS
    factor = HEAD_DIM ** -0.5
    query_blocks = queries.reshape(STEPS, N_REPLICA, ROWS, D).transpose(1, 0, 2, 3)
    fresh_blocks = new_entries.reshape(STEPS, N_REPLICA, ROWS, KV_HEADS, 2 * HEAD_DIM).transpose(1, 0, 2, 3, 4)
    cache_blocks = cache.reshape(N_REPLICA, ROWS, KV_HEADS, CACHE, 2 * HEAD_DIM)
    length_blocks = lengths.reshape(N_REPLICA, ROWS)
    page_blocks = page_index.reshape(N_REPLICA, ROWS)

    def one_block(inputs):
        query_part, fresh_part, cache_part, length_part, page_part = inputs
        grouped = query_part.astype(jnp.float32).reshape(STEPS, ROWS, KV_HEADS, query_group_width, HEAD_DIM)
        key_part = cache_part[..., :HEAD_DIM].astype(jnp.float32)
        value_part = cache_part[..., HEAD_DIM:].astype(jnp.float32)
        new_keys = fresh_part[..., :HEAD_DIM].astype(jnp.float32)
        new_values = fresh_part[..., HEAD_DIM:].astype(jnp.float32)
        cache_scores = jnp.einsum("srkgd,rkld->srkgl", grouped, key_part) * factor
        positions = jnp.arange(CACHE, dtype=jnp.int32)
        visible = (positions[None, :] < length_part[:, None])[None, :, None, None, :]
        cache_scores = jnp.where(visible, cache_scores, neg_large)
        fresh_scores = jnp.einsum("srkgd,jrkd->srkgj", grouped, new_keys) * factor
        step_ids = jnp.arange(STEPS, dtype=jnp.int32)
        causal = (step_ids[:, None] >= step_ids[None, :])[:, None, None, None, :]
        fresh_scores = jnp.where(causal, fresh_scores, neg_large)
        top = jnp.maximum(jnp.max(cache_scores, axis=-1), jnp.max(fresh_scores, axis=-1))
        cache_weights = jnp.where(visible, jnp.exp(cache_scores - top[..., None]), 0.0)
        fresh_weights = jnp.where(causal, jnp.exp(fresh_scores - top[..., None]), 0.0)
        total = jnp.sum(cache_weights, axis=-1) + jnp.sum(fresh_weights, axis=-1)
        cache_round = lax.optimization_barrier(cache_weights.astype(jnp.bfloat16)).astype(jnp.float32)
        fresh_round = lax.optimization_barrier(fresh_weights.astype(jnp.bfloat16)).astype(jnp.float32)
        accum = jnp.einsum("srkgl,rkld->srkgd", cache_round, value_part)
        accum = accum + jnp.einsum("srkgj,jrkd->srkgd", fresh_round, new_values)
        attended = (accum / total[..., None]).reshape(STEPS, ROWS, D).astype(jnp.bfloat16)
        selected_adapter = adapter_pages[page_part].astype(jnp.float32)
        down_projection = jnp.einsum("srd,rkd->srk", attended.astype(jnp.float32), selected_adapter[:, 0])
        down_projection = lax.optimization_barrier(down_projection.astype(jnp.bfloat16)).astype(jnp.float32)
        adapted = (jnp.einsum("vew,ewl->vel", down_projection, selected_adapter[:, 1]) * adapter_scale).astype(jnp.bfloat16)
        return attended, adapted

    attended, adapted = lax.map(one_block, (query_blocks, fresh_blocks, cache_blocks, length_blocks, page_blocks))
    attended = attended.transpose(1, 0, 2, 3).reshape(STEPS, ROWS_TOTAL, D)
    adapted = adapted.transpose(1, 0, 2, 3).reshape(STEPS, ROWS_TOTAL, D)
    return attended, adapted
```

```python
import jax
import jax.numpy as jnp
from jax import lax
from jax.experimental import pallas as pl
from jax.experimental.pallas import tpu as pltpu
from jax.sharding import PartitionSpec as P

f32 = jnp.float32
bf16 = jnp.bfloat16

X_SIZE = 4
SLOTS = 8
ADAPTER_SCALE = 0.5
NEG_LARGE = -1e30
LANES = 128


def vmem_spec():
    return pl.BlockSpec(memory_space=pltpu.VMEM)


def smem_spec():
    return pl.BlockSpec(memory_space=pltpu.SMEM)


def params():
    return pltpu.CompilerParams(vmem_limit_bytes=32 * 1024 * 1024)


def iota(shape, axis):
    return lax.broadcasted_iota(jnp.int32, shape, axis)


def attention_kernel(lengths_ref, q_ref, new_ref, cache_ref, out_ref, q_rows):
    steps, rows, width = q_ref.shape
    kv_heads, local = cache_ref.shape[1], cache_ref.shape[2]
    head = cache_ref.shape[3] // 2
    group = width // head // kv_heads
    tensor_here = lax.axis_index("tensor")
    sr = steps * rows
    count = group * sr
    for s in range(steps):
        q_rows[s * rows : (s + 1) * rows, :] = q_ref[s].astype(f32)
    new_all = new_ref[...].astype(f32).reshape(steps * rows * kv_heads, 2 * head).astype(bf16)
    new_keys, new_values = new_all[:, :head], new_all[:, head:]
    shape = (count, rows * local)
    row_id, col_id = iota(shape, 0), iota(shape, 1)
    request, step = row_id % rows, (row_id // rows) % steps
    col_request = col_id // local
    length = jnp.zeros(shape, jnp.int32)
    for r in range(rows):
        length = jnp.where(col_request == r, lengths_ref[r], length)
    visible = (request == col_request) & (tensor_here * local + col_id % local < length)
    fresh_shape = (count, steps * rows * kv_heads)
    fresh_col = iota(fresh_shape, 1)
    fresh_row = iota(fresh_shape, 0)
    fresh = (
        (fresh_row % rows == (fresh_col // kv_heads) % rows)
        & (fresh_col // (kv_heads * rows) <= (fresh_row // rows) % steps)
        & (tensor_here == 0)
    )
    fresh_head = fresh_col % kv_heads
    factor = head ** (-0.5)
    contract = (((1,), (1,)), ((), ()))
    lane = iota((sr, LANES), 1)
    per_tile = out_ref.shape[2] // head - 1
    for g in range(kv_heads):
        q = jnp.concatenate(
            [q_rows[:, (g * group + k) * head : (g * group + k + 1) * head] for k in range(group)],
            axis=0,
        ).astype(bf16)
        keys = cache_ref[:, g, :, :head].reshape(rows * local, head)
        values = cache_ref[:, g, :, head:].reshape(rows * local, head)
        fresh_here = fresh & (fresh_head == g)
        old_scores = lax.dot_general(q, keys, contract, preferred_element_type=f32) * factor
        new_scores = lax.dot_general(q, new_keys, contract, preferred_element_type=f32) * factor
        old_scores = jnp.where(visible, old_scores, NEG_LARGE)
        new_scores = jnp.where(fresh_here, new_scores, NEG_LARGE)
        top = jnp.max(jnp.maximum(old_scores, new_scores), axis=1, keepdims=True)
        shift = top.astype(bf16).astype(f32)
        old_weights = jnp.where(visible, jnp.exp(old_scores - shift), 0.0)
        new_weights = jnp.where(fresh_here, jnp.exp(new_scores - shift), 0.0)
        total = jnp.sum(old_weights + new_weights, axis=1, keepdims=True)
        accum = jnp.dot(old_weights.astype(bf16), values, preferred_element_type=f32)
        accum = accum + jnp.dot(new_weights.astype(bf16), new_values, preferred_element_type=f32)
        high = total.astype(bf16).astype(f32)
        low = total - high
        for first in range(0, group, per_tile):
            place = (g * group + first) // per_tile
            stats = jnp.zeros((sr, LANES), f32)
            for k in range(per_tile):
                part = slice((first + k) * sr, (first + k + 1) * sr)
                out_ref[place, :, k * head : (k + 1) * head] = accum[part].astype(bf16)
                stats = jnp.where(lane == k, shift[part], stats)
                stats = jnp.where(lane == per_tile + k, high[part], stats)
                stats = jnp.where(lane == 2 * per_tile + k, low[part], stats)
            out_ref[place, :, per_tile * head :] = stats.astype(bf16)


def combine_kernel(slots_ref, source_ref, source_slot_ref, part_ref, attended_ref, send_ref):
    steps, rows, width = attended_ref.shape
    sources = part_ref.shape[0]
    per_tile = width // LANES
    stats = [part_ref[t, :, width:].astype(f32) for t in range(sources)]
    top = stats[0]
    for t in range(1, sources):
        top = jnp.maximum(top, stats[t])
    sums = [jnp.zeros((steps * rows, LANES), f32) for _ in range(per_tile)]
    total = jnp.zeros((steps * rows, LANES), f32)
    for t in range(sources):
        fade = jnp.exp(stats[t] - top)
        both = pltpu.roll(stats[t], LANES - per_tile, 1) + pltpu.roll(
            stats[t], LANES - 2 * per_tile, 1
        )
        total = total + fade * both
        for k in range(per_tile):
            sums[k] = sums[k] + fade[:, k : k + 1] * part_ref[
                t, :, k * LANES : (k + 1) * LANES
            ].astype(f32)
    replica_here = lax.axis_index("replica")
    row = iota((steps * rows, LANES), 0) % rows
    page = jnp.zeros((steps * rows, LANES), f32)
    for r in range(rows):
        slot = slots_ref[r]
        entry = jnp.clip(slot - SLOTS, 0, source_slot_ref.shape[0] - 1)
        number = jnp.where(
            slot < SLOTS,
            replica_here * SLOTS + slot,
            source_ref[entry] * SLOTS + source_slot_ref[entry],
        )
        page = jnp.where(row == r, number.astype(f32), page)
    page = page.astype(bf16)
    for k in range(per_tile):
        attended = sums[k] / total[:, k : k + 1]
        for s in range(steps):
            attended_ref[s, :, k * LANES : (k + 1) * LANES] = attended[
                s * rows : (s + 1) * rows
            ].astype(bf16)
        rounded = attended.astype(bf16)
        for z in range(send_ref.shape[0]):
            send_ref[z, :, k * LANES : (k + 1) * LANES] = rounded
    for z in range(send_ref.shape[0]):
        send_ref[z, :, width:] = page


def page_columns(page, first, rank, width):
    return page[:, :1] == (first + iota((page.shape[0], width), 1) // rank).astype(f32)


def shrink_kernel(rows_ref, shrink_ref, out_ref):
    z_count, rows, padded = rows_ref.shape
    pages, rank, width = shrink_ref.shape
    count = z_count * rows
    at_once = 256 // rank
    data = rows_ref[...].reshape(count, padded)
    x, page = data[:, :width], data[:, width:].astype(f32)
    base = lax.axis_index("replica") // X_SIZE * (X_SIZE * SLOTS)
    accum = jnp.zeros((count, at_once * rank), f32)
    for p in range(0, pages, at_once):
        block = shrink_ref[p : p + at_once].reshape(at_once * rank, width)
        product = lax.dot_general(x, block, (((1,), (1,)), ((), ())), preferred_element_type=f32)
        accum = accum + jnp.where(
            page_columns(page, base + p, rank, at_once * rank), product, 0.0
        )
    folded = accum[:, :LANES] + accum[:, LANES:]
    folded = folded + pltpu.roll(folded, rank, 1)
    half = count // 2
    packed = jnp.where(iota((half, LANES), 1) < rank, folded[:half], folded[half:]).astype(bf16)
    for t in range(out_ref.shape[0]):
        out_ref[t] = packed


def expand_kernel(part_ref, rows_ref, expand_ref, out_ref):
    z_count, rows, padded = rows_ref.shape
    pages, rank, width = expand_ref.shape
    count = z_count * rows
    at_once = 256 // rank
    page = rows_ref[:, :, width:].reshape(count, padded - width).astype(f32)
    base = lax.axis_index("replica") // X_SIZE * (X_SIZE * SLOTS)
    packed = part_ref[0].astype(f32)
    for t in range(1, part_ref.shape[0]):
        packed = packed + part_ref[t].astype(f32)
    swapped = pltpu.roll(packed, rank, 1)
    left = iota(packed.shape, 1) < rank
    low = jnp.concatenate(
        [jnp.where(left, packed, swapped), jnp.where(left, swapped, packed)], axis=0
    )
    low = jnp.concatenate([low, low], axis=1).astype(bf16).astype(f32)
    accum = jnp.zeros((count, width), f32)
    for p in range(0, pages, at_once):
        block = expand_ref[p : p + at_once].reshape(at_once * rank, width)
        used = jnp.where(page_columns(page, base + p, rank, at_once * rank), low, 0.0)
        accum = accum + jnp.dot(used.astype(bf16), block, preferred_element_type=f32)
    out_ref[...] = (accum * ADAPTER_SCALE).astype(bf16).reshape(z_count, rows, width)


def gather_kernel(part_ref, out_ref):
    steps, rows, _ = out_ref.shape
    total = part_ref[0].astype(f32)
    for z in range(1, part_ref.shape[0]):
        total = total + part_ref[z].astype(f32)
    for s in range(steps):
        out_ref[s] = total[s * rows : (s + 1) * rows].astype(bf16)


def per_device(
    queries, new_entries, cache, lengths, adapter_pages, request_slots, source_replica, source_slot
):
    replicas, tensors = lax.axis_size("replica"), lax.axis_size("tensor")
    z_size = replicas // X_SIZE
    x_groups = [[z * X_SIZE + x for x in range(X_SIZE)] for z in range(z_size)]
    z_groups = [[z * X_SIZE + x for z in range(z_size)] for x in range(X_SIZE)]
    steps, rows, model = queries.shape
    width = model // tensors
    rank = adapter_pages.shape[2]
    pages = X_SIZE * adapter_pages.shape[0]
    sr = steps * rows
    count = z_size * sr

    shrink_pages = lax.all_gather(
        adapter_pages[:, 0], "replica", axis_index_groups=x_groups, tiled=True
    )
    expand_pages = lax.all_gather(
        adapter_pages[:, 1], "replica", axis_index_groups=x_groups, tiled=True
    )

    parts = pl.pallas_call(
        attention_kernel,
        out_shape=jax.ShapeDtypeStruct((tensors, sr, width + LANES), bf16),
        in_specs=[smem_spec(), vmem_spec(), vmem_spec(), vmem_spec()],
        out_specs=vmem_spec(),
        scratch_shapes=[pltpu.VMEM((sr, model), f32)],
        compiler_params=params(),
        name="attention_part",
    )(lengths, queries, new_entries, cache)
    parts = lax.all_to_all(parts, "tensor", 0, 0, tiled=True)

    attended, outgoing = pl.pallas_call(
        combine_kernel,
        out_shape=(
            jax.ShapeDtypeStruct((steps, rows, width), bf16),
            jax.ShapeDtypeStruct((z_size, sr, width + LANES), bf16),
        ),
        in_specs=[smem_spec(), smem_spec(), smem_spec(), vmem_spec()],
        out_specs=(vmem_spec(), vmem_spec()),
        compiler_params=params(),
        name="combine",
    )(request_slots, source_replica[:, 0], source_slot, parts)
    column = lax.all_to_all(
        outgoing, "replica", 0, 0, tiled=True, axis_index_groups=z_groups
    )

    low = pl.pallas_call(
        shrink_kernel,
        out_shape=jax.ShapeDtypeStruct((tensors, count // 2, LANES), bf16),
        in_specs=[vmem_spec(), vmem_spec()],
        out_specs=vmem_spec(),
        compiler_params=params(),
        name="shrink_part",
    )(column, shrink_pages)
    low = lax.all_to_all(low, "tensor", 0, 0, tiled=True)

    back = pl.pallas_call(
        expand_kernel,
        out_shape=jax.ShapeDtypeStruct((z_size, sr, width), bf16),
        in_specs=[vmem_spec(), vmem_spec(), vmem_spec()],
        out_specs=vmem_spec(),
        compiler_params=params(),
        name="expand_rows",
    )(low, column, expand_pages)
    back = lax.all_to_all(back, "replica", 0, 0, tiled=True, axis_index_groups=z_groups)

    adapted = pl.pallas_call(
        gather_kernel,
        out_shape=jax.ShapeDtypeStruct((steps, rows, width), bf16),
        in_specs=[vmem_spec()],
        out_specs=vmem_spec(),
        compiler_params=params(),
        name="returned_rows",
    )(back)
    return attended, adapted


def solution(mesh):
    return jax.shard_map(
        per_device,
        mesh=mesh,
        in_specs=(
            P(None, "replica", None),
            P(None, "replica", None, None),
            P("replica", None, "tensor", None),
            P("replica"),
            P("replica", None, None, "tensor"),
            P("replica"),
            P("replica", None),
            P("replica"),
        ),
        out_specs=(P(None, "replica", "tensor"), P(None, "replica", "tensor")),
        check_vma=False,
    )
```

```python
import jax
import jax.numpy as jnp
from jax import lax
from jax.experimental import pallas as pl
from jax.experimental.pallas import tpu as pltpu
from jax.sharding import PartitionSpec as P

f32 = jnp.float32
bf16 = jnp.bfloat16

X_SIZE = 4
SLOTS = 8
ADAPTER_SCALE = 0.5
NEG_LARGE = -1e30
LANES = 128
HELD = ((0, 0), (1, 0), (3, 0), (2, 0), (2, SLOTS // 2))


def vmem_spec():
    return pl.BlockSpec(memory_space=pltpu.VMEM)


def smem_spec():
    return pl.BlockSpec(memory_space=pltpu.SMEM)


def params():
    return pltpu.CompilerParams(vmem_limit_bytes=32 * 1024 * 1024)


def iota(shape, axis):
    return lax.broadcasted_iota(jnp.int32, shape, axis)


def attention_kernel(lengths_ref, q_ref, new_ref, cache_ref, out_ref, q_rows):
    steps, rows, width = q_ref.shape
    kv_heads, local = cache_ref.shape[1], cache_ref.shape[2]
    head = cache_ref.shape[3] // 2
    group = width // head // kv_heads
    tensor_here = lax.axis_index("tensor")
    sr = steps * rows
    count = group * sr
    for s in range(steps):
        q_rows[s * rows : (s + 1) * rows, :] = q_ref[s].astype(f32)
    new_all = new_ref[...].astype(f32).reshape(steps * rows * kv_heads, 2 * head).astype(bf16)
    new_keys, new_values = new_all[:, :head], new_all[:, head:]
    shape = (count, rows * local)
    row_id, col_id = iota(shape, 0), iota(shape, 1)
    request, step = row_id % rows, (row_id // rows) % steps
    col_request = col_id // local
    length = jnp.zeros(shape, jnp.int32)
    for r in range(rows):
        length = jnp.where(col_request == r, lengths_ref[r], length)
    visible = (request == col_request) & (tensor_here * local + col_id % local < length)
    fresh_shape = (count, steps * rows * kv_heads)
    fresh_col = iota(fresh_shape, 1)
    fresh_row = iota(fresh_shape, 0)
    fresh = (
        (fresh_row % rows == (fresh_col // kv_heads) % rows)
        & (fresh_col // (kv_heads * rows) <= (fresh_row // rows) % steps)
        & (tensor_here == 0)
    )
    fresh_head = fresh_col % kv_heads
    factor = head ** (-0.5)
    contract = (((1,), (1,)), ((), ()))
    lane = iota((sr, LANES), 1)
    per_tile = out_ref.shape[2] // head - 1
    for g in range(kv_heads):
        q = jnp.concatenate(
            [q_rows[:, (g * group + k) * head : (g * group + k + 1) * head] for k in range(group)],
            axis=0,
        ).astype(bf16)
        keys = cache_ref[:, g, :, :head].reshape(rows * local, head)
        values = cache_ref[:, g, :, head:].reshape(rows * local, head)
        fresh_here = fresh & (fresh_head == g)
        old_scores = lax.dot_general(q, keys, contract, preferred_element_type=f32) * factor
        new_scores = lax.dot_general(q, new_keys, contract, preferred_element_type=f32) * factor
        old_scores = jnp.where(visible, old_scores, NEG_LARGE)
        new_scores = jnp.where(fresh_here, new_scores, NEG_LARGE)
        top = jnp.max(jnp.maximum(old_scores, new_scores), axis=1, keepdims=True)
        shift = top.astype(bf16).astype(f32)
        old_weights = jnp.where(visible, jnp.exp(old_scores - shift), 0.0)
        new_weights = jnp.where(fresh_here, jnp.exp(new_scores - shift), 0.0)
        total = jnp.sum(old_weights + new_weights, axis=1, keepdims=True)
        accum = jnp.dot(old_weights.astype(bf16), values, preferred_element_type=f32)
        accum = accum + jnp.dot(new_weights.astype(bf16), new_values, preferred_element_type=f32)
        high = total.astype(bf16).astype(f32)
        low = total - high
        for first in range(0, group, per_tile):
            place = (g * group + first) // per_tile
            stats = jnp.zeros((sr, LANES), f32)
            for k in range(per_tile):
                part = slice((first + k) * sr, (first + k + 1) * sr)
                out_ref[place, :, k * head : (k + 1) * head] = accum[part].astype(bf16)
                stats = jnp.where(lane == k, shift[part], stats)
                stats = jnp.where(lane == per_tile + k, high[part], stats)
                stats = jnp.where(lane == 2 * per_tile + k, low[part], stats)
            out_ref[place, :, per_tile * head :] = stats.astype(bf16)


def combine_kernel(slots_ref, source_ref, source_slot_ref, part_ref, attended_ref, send_ref):
    steps, rows, width = attended_ref.shape
    sources = part_ref.shape[0]
    per_tile = width // LANES
    stats = [part_ref[t, :, width:].astype(f32) for t in range(sources)]
    top = stats[0]
    for t in range(1, sources):
        top = jnp.maximum(top, stats[t])
    sums = [jnp.zeros((steps * rows, LANES), f32) for _ in range(per_tile)]
    total = jnp.zeros((steps * rows, LANES), f32)
    for t in range(sources):
        fade = jnp.exp(stats[t] - top)
        both = pltpu.roll(stats[t], LANES - per_tile, 1) + pltpu.roll(
            stats[t], LANES - 2 * per_tile, 1
        )
        total = total + fade * both
        for k in range(per_tile):
            sums[k] = sums[k] + fade[:, k : k + 1] * part_ref[
                t, :, k * LANES : (k + 1) * LANES
            ].astype(f32)
    replica_here = lax.axis_index("replica")
    row = iota((steps * rows, LANES), 0) % rows
    page = jnp.zeros((steps * rows, LANES), f32)
    for r in range(rows):
        slot = slots_ref[r]
        entry = jnp.clip(slot - SLOTS, 0, source_slot_ref.shape[0] - 1)
        number = jnp.where(
            slot < SLOTS,
            replica_here * SLOTS + slot,
            source_ref[entry] * SLOTS + source_slot_ref[entry],
        )
        page = jnp.where(row == r, number.astype(f32), page)
    page = page.astype(bf16)
    for k in range(per_tile):
        attended = sums[k] / total[:, k : k + 1]
        for s in range(steps):
            attended_ref[s, :, k * LANES : (k + 1) * LANES] = attended[
                s * rows : (s + 1) * rows
            ].astype(bf16)
        rounded = attended.astype(bf16)
        for z in range(send_ref.shape[0]):
            send_ref[z, :, k * LANES : (k + 1) * LANES] = rounded
    for z in range(send_ref.shape[0]):
        send_ref[z, :, width:] = page


def page_columns(page, first, rank, width):
    return page[:, :1] == (first + iota((page.shape[0], width), 1) // rank).astype(f32)


def page_blocks(refs, half, at_once):
    replica_here = lax.axis_index("replica")
    z_here, x_here = replica_here // X_SIZE, replica_here % X_SIZE
    for ref, (distance, start) in zip(refs, HELD):
        owner = z_here * X_SIZE + jnp.bitwise_xor(x_here, distance)
        for p in range(0, ref.shape[0], at_once):
            block = ref[p : p + at_once, half]
            yield owner * SLOTS + start + p, block.reshape(at_once * block.shape[1], block.shape[2])


def shrink_kernel(rows_ref, *refs):
    page_refs, out_ref = refs[:-1], refs[-1]
    z_count, rows, padded = rows_ref.shape
    rank, width = page_refs[0].shape[2:]
    count = z_count * rows
    at_once = 256 // rank
    data = rows_ref[...].reshape(count, padded)
    x, page = data[:, :width], data[:, width:].astype(f32)
    accum = jnp.zeros((count, at_once * rank), f32)
    for first, block in page_blocks(page_refs, 0, at_once):
        product = lax.dot_general(x, block, (((1,), (1,)), ((), ())), preferred_element_type=f32)
        accum = accum + jnp.where(page_columns(page, first, rank, at_once * rank), product, 0.0)
    folded = accum[:, :LANES] + accum[:, LANES:]
    folded = folded + pltpu.roll(folded, rank, 1)
    half = count // 2
    packed = jnp.where(iota((half, LANES), 1) < rank, folded[:half], folded[half:]).astype(bf16)
    for t in range(out_ref.shape[0]):
        out_ref[t] = packed


def expand_kernel(part_ref, rows_ref, *refs):
    page_refs, out_ref = refs[:-1], refs[-1]
    z_count, rows, padded = rows_ref.shape
    rank, width = page_refs[0].shape[2:]
    count = z_count * rows
    at_once = 256 // rank
    page = rows_ref[:, :, width:].reshape(count, padded - width).astype(f32)
    packed = part_ref[0].astype(f32)
    for t in range(1, part_ref.shape[0]):
        packed = packed + part_ref[t].astype(f32)
    swapped = pltpu.roll(packed, rank, 1)
    left = iota(packed.shape, 1) < rank
    low = jnp.concatenate(
        [jnp.where(left, packed, swapped), jnp.where(left, swapped, packed)], axis=0
    )
    low = jnp.concatenate([low, low], axis=1).astype(bf16).astype(f32)
    accum = jnp.zeros((count, width), f32)
    for first, block in page_blocks(page_refs, 1, at_once):
        used = jnp.where(page_columns(page, first, rank, at_once * rank), low, 0.0)
        accum = accum + jnp.dot(used.astype(bf16), block, preferred_element_type=f32)
    out_ref[...] = (accum * ADAPTER_SCALE).astype(bf16).reshape(z_count, rows, width)


def gather_kernel(part_ref, out_ref):
    steps, rows, _ = out_ref.shape
    total = part_ref[0].astype(f32)
    for z in range(1, part_ref.shape[0]):
        total = total + part_ref[z].astype(f32)
    for s in range(steps):
        out_ref[s] = total[s * rows : (s + 1) * rows].astype(bf16)


def per_device(
    queries, new_entries, cache, lengths, adapter_pages, request_slots, source_replica, source_slot
):
    replicas, tensors = lax.axis_size("replica"), lax.axis_size("tensor")
    z_size = replicas // X_SIZE
    z_groups = [[z * X_SIZE + x for z in range(z_size)] for x in range(X_SIZE)]
    steps, rows, model = queries.shape
    width = model // tensors
    rank = adapter_pages.shape[2]
    sr = steps * rows
    count = z_size * sr

    def exchange(array, distance):
        pairs = [(i, i // X_SIZE * X_SIZE + (i % X_SIZE ^ distance)) for i in range(replicas)]
        return lax.ppermute(array, "replica", pairs)

    beside = exchange(adapter_pages, 1)
    before = exchange(adapter_pages, 3)

    parts = pl.pallas_call(
        attention_kernel,
        out_shape=jax.ShapeDtypeStruct((tensors, sr, width + LANES), bf16),
        in_specs=[smem_spec(), vmem_spec(), vmem_spec(), vmem_spec()],
        out_specs=vmem_spec(),
        scratch_shapes=[pltpu.VMEM((sr, model), f32)],
        compiler_params=params(),
        name="attention_part",
    )(lengths, queries, new_entries, cache)
    parts = lax.all_to_all(parts, "tensor", 0, 0, tiled=True)

    half = SLOTS // 2
    beside, before, _ = lax.optimization_barrier((beside, before, parts))
    held = (
        adapter_pages,
        beside,
        before,
        exchange(before[:half], 1),
        exchange(beside[half:], 3),
    )

    attended, outgoing = pl.pallas_call(
        combine_kernel,
        out_shape=(
            jax.ShapeDtypeStruct((steps, rows, width), bf16),
            jax.ShapeDtypeStruct((z_size, sr, width + LANES), bf16),
        ),
        in_specs=[smem_spec(), smem_spec(), smem_spec(), vmem_spec()],
        out_specs=(vmem_spec(), vmem_spec()),
        compiler_params=params(),
        name="combine",
    )(request_slots, source_replica[:, 0], source_slot, parts)
    column = lax.all_to_all(
        outgoing, "replica", 0, 0, tiled=True, axis_index_groups=z_groups
    )

    low = pl.pallas_call(
        shrink_kernel,
        out_shape=jax.ShapeDtypeStruct((tensors, count // 2, LANES), bf16),
        in_specs=[vmem_spec()] * (1 + len(held)),
        out_specs=vmem_spec(),
        compiler_params=params(),
        name="shrink_part",
    )(column, *held)
    low = lax.all_to_all(low, "tensor", 0, 0, tiled=True)

    back = pl.pallas_call(
        expand_kernel,
        out_shape=jax.ShapeDtypeStruct((z_size, sr, width), bf16),
        in_specs=[vmem_spec()] * (2 + len(held)),
        out_specs=vmem_spec(),
        compiler_params=params(),
        name="expand_rows",
    )(low, column, *held)
    back = lax.all_to_all(back, "replica", 0, 0, tiled=True, axis_index_groups=z_groups)

    adapted = pl.pallas_call(
        gather_kernel,
        out_shape=jax.ShapeDtypeStruct((steps, rows, width), bf16),
        in_specs=[vmem_spec()],
        out_specs=vmem_spec(),
        compiler_params=params(),
        name="returned_rows",
    )(back)
    return attended, adapted


def solution(mesh):
    return jax.shard_map(
        per_device,
        mesh=mesh,
        in_specs=(
            P(None, "replica", None),
            P(None, "replica", None, None),
            P("replica", None, "tensor", None),
            P("replica"),
            P("replica", None, None, "tensor"),
            P("replica"),
            P("replica", None),
            P("replica"),
        ),
        out_specs=(P(None, "replica", "tensor"), P(None, "replica", "tensor")),
        check_vma=False,
    )
```

```python
import jax
import jax.numpy as jnp
from jax import lax
from jax.experimental import pallas as pl
from jax.experimental.pallas import tpu as pltpu
from jax.sharding import PartitionSpec as P

f32 = jnp.float32
bf16 = jnp.bfloat16

X_SIZE = 4
SLOTS = 8
ADAPTER_SCALE = 0.5
NEG_LARGE = -1e30
LANES = 128
LOG2_E = 1.4426950408889634
BLOCK = (0, 1, 3, 2)
ROWS = 4
AT_ONCE = 16


def vmem_spec():
    return pl.BlockSpec(memory_space=pltpu.VMEM)


def hbm_spec():
    return pl.BlockSpec(memory_space=pltpu.HBM)


def in_hbm(array):
    return pltpu.with_memory_space_constraint(array, pltpu.HBM)


def smem_spec():
    return pl.BlockSpec(memory_space=pltpu.SMEM)


def params():
    return pltpu.CompilerParams(vmem_limit_bytes=8 * 1024 * 1024)


def iota(shape, axis):
    return lax.broadcasted_iota(jnp.int32, shape, axis)


def attention_kernel(
    lengths_hbm,
    q_hbm,
    new_hbm,
    cache_hbm,
    out_hbm,
    lengths_ref,
    q_ref,
    new_ref,
    cache_ref,
    q_rows,
    out_ref,
    arrived,
    sent,
):
    copies = [
        pltpu.make_async_copy(q_hbm, q_ref, arrived.at[0]),
        pltpu.make_async_copy(new_hbm, new_ref, arrived.at[1]),
        pltpu.make_async_copy(lengths_hbm, lengths_ref, arrived.at[2]),
    ]
    cache_copies = [
        pltpu.make_async_copy(cache_hbm.at[:, g], cache_ref.at[g], arrived.at[3 + g])
        for g in range(cache_ref.shape[0])
    ]
    for copy in copies + cache_copies:
        copy.start()
    steps, rows, width = q_ref.shape
    kv_heads, local = cache_ref.shape[0], cache_ref.shape[2]
    head = cache_ref.shape[3] // 2
    group = width // head // kv_heads
    tensor_here = lax.axis_index("tensor")
    sr = steps * rows
    count = group * sr
    shape = (count, rows * local)
    row_id, col_id = iota(shape, 0), iota(shape, 1)
    request, col_request = row_id % rows, col_id // local
    fresh_shape = (count, steps * rows * kv_heads)
    fresh_row, fresh_col = iota(fresh_shape, 0), iota(fresh_shape, 1)
    fresh = (
        (fresh_row % rows == (fresh_col // kv_heads) % rows)
        & (fresh_col // (kv_heads * rows) <= (fresh_row // rows) % steps)
        & (tensor_here == 0)
    )
    fresh_head = jnp.where(fresh, fresh_col % kv_heads, -1)
    lane = iota((sr, LANES), 1)
    per_tile = out_ref.shape[2] // head - 1
    field = LANES // 2 // per_tile
    factor = head ** (-0.5) * LOG2_E
    contract = (((1,), (1,)), ((), ()))
    for copy in copies + cache_copies:
        copy.wait()
    length = jnp.zeros(shape, jnp.int32)
    for r in range(rows):
        length = jnp.where(col_request == r, lengths_ref[r], length)
    visible = (request == col_request) & (tensor_here * local + col_id % local < length)
    for s in range(steps):
        q_rows[s * rows : (s + 1) * rows, :] = q_ref[s].astype(f32)
    new_all = new_ref[...].astype(f32).reshape(steps * rows * kv_heads, 2 * head).astype(bf16)
    new_keys, new_values = new_all[:, :head], new_all[:, head:]
    ones = jnp.ones((rows * local + new_keys.shape[0], head), bf16)
    out_copies = []
    for g in range(kv_heads):
        q = jnp.concatenate(
            [q_rows[:, (g * group + k) * head : (g * group + k + 1) * head] for k in range(group)],
            axis=0,
        ).astype(bf16)
        keys = cache_ref[g, :, :, :head].reshape(rows * local, head)
        values = cache_ref[g, :, :, head:].reshape(rows * local, head)
        keys = jnp.concatenate([keys, new_keys], axis=0)
        values = jnp.concatenate([values, new_values], axis=0)
        values = jnp.concatenate([values, ones], axis=1)
        scores = lax.dot_general(q, keys, contract, preferred_element_type=f32) * factor
        old_scores = jnp.where(visible, scores[:, : rows * local], NEG_LARGE)
        new_scores = jnp.where(fresh_head == g, scores[:, rows * local :], NEG_LARGE)
        top = jnp.max(jnp.maximum(old_scores, new_scores), axis=1, keepdims=True)
        shift = jnp.maximum(top, 0.01 * NEG_LARGE).astype(bf16).astype(f32)
        weights = jnp.concatenate(
            [jnp.exp2(old_scores - shift), jnp.exp2(new_scores - shift)], axis=1
        ).astype(bf16)
        sums = jnp.dot(weights, values, preferred_element_type=f32)
        accum, total = sums[:, :head], sums[:, head:]
        for first in range(0, group, per_tile):
            place = (g * group + first) // per_tile
            stats = jnp.zeros((sr, LANES), f32)
            for k in range(per_tile):
                part = slice((first + k) * sr, (first + k + 1) * sr)
                out_ref[place, :, k * head : (k + 1) * head] = accum[part].astype(bf16)
                stats = jnp.where(lane // field == k, shift[part], stats)
                stats = jnp.where(lane // field == per_tile + k, total[part], stats)
            out_ref[place, :, per_tile * head :] = stats.astype(bf16)
        places = group // per_tile
        here = pl.ds(g * places, places)
        out_copies.append(
            pltpu.make_async_copy(out_ref.at[here], out_hbm.at[here], sent.at[g])
        )
        out_copies[-1].start()
    for copy in out_copies:
        copy.wait()


def send_all(ref, hbm, sent):
    copies = [
        pltpu.make_async_copy(ref, hbm.at[i], sent.at[i]) for i in range(hbm.shape[0])
    ]
    for copy in copies:
        copy.start()
    for copy in copies:
        copy.wait()


def combine_kernel(slots_ref, source_ref, source_slot_ref, part_ref, attended_ref, send_hbm, send_ref, sent):
    steps, rows, width = attended_ref.shape
    sources = part_ref.shape[0]
    per_tile = width // LANES
    field = LANES // 2 // per_tile
    stats = [part_ref[t, :, width:].astype(f32) for t in range(sources)]
    top = stats[0]
    for t in range(1, sources):
        top = jnp.maximum(top, stats[t])
    sums = [jnp.zeros((steps * rows, LANES), f32) for _ in range(per_tile)]
    total = jnp.zeros((steps * rows, LANES), f32)
    for t in range(sources):
        fade = jnp.exp2(stats[t] - top)
        total = total + fade * pltpu.roll(stats[t], LANES // 2, 1)
        for k in range(per_tile):
            sums[k] = sums[k] + fade[:, k * field : k * field + 1] * part_ref[
                t, :, k * LANES : (k + 1) * LANES
            ].astype(f32)
    replica_here = lax.axis_index("replica")
    row = iota((steps * rows, LANES), 0) % rows
    page = jnp.zeros((steps * rows, LANES), f32)
    for r in range(rows):
        slot = slots_ref[r]
        entry = jnp.clip(slot - SLOTS, 0, source_slot_ref.shape[0] - 1)
        number = jnp.where(
            slot < SLOTS,
            replica_here * SLOTS + slot,
            source_ref[entry] * SLOTS + source_slot_ref[entry],
        )
        page = jnp.where(row == r, number.astype(f32), page)
    page = page.astype(bf16)
    for k in range(per_tile):
        attended = sums[k] / total[:, k * field : k * field + 1]
        for s in range(steps):
            attended_ref[s, :, k * LANES : (k + 1) * LANES] = attended[
                s * rows : (s + 1) * rows
            ].astype(bf16)
        rounded = attended.astype(bf16)
        send_ref[:, k * LANES : (k + 1) * LANES] = rounded
    send_ref[:, width:] = page
    send_all(send_ref, send_hbm, sent)


def page_columns(page, first, rank, width):
    return page[:, :1] == (first + iota((page.shape[0], width), 1) // rank).astype(f32)


def page_blocks(refs, at_once):
    replica_here = lax.axis_index("replica")
    for distance, ref in zip(BLOCK, refs):
        first = jnp.bitwise_xor(replica_here, distance) * SLOTS
        for p in range(0, ref.shape[0], at_once):
            block = ref[p : p + at_once]
            yield first + p, block.reshape(at_once * block.shape[1], block.shape[2])


def shrink_kernel(
    turn_ref,
    rows_ref,
    *refs,
):
    members, steps_rows, padded = rows_ref.shape
    page_refs = refs[: len(BLOCK)]
    out_hbm, place_ref, chosen_ref, count_ref, out_ref, sent = refs[len(BLOCK) :]
    rank, width = page_refs[0].shape[1:]
    count = members * steps_rows
    rows = ROWS
    steps = steps_rows // rows
    data = rows_ref[...].reshape(count, padded)
    x, page = data[:, :width], data[:, width:].astype(f32)
    distance = jnp.bitwise_xor(page.astype(jnp.int32) // SLOTS, lax.axis_index("replica"))
    held = distance == BLOCK[0]
    for other in BLOCK[1:]:
        held = held | (distance == other)
    held = held.astype(f32)
    one, other = iota((count, count), 0), iota((count, count), 1)
    earlier = (
        (other // steps_rows * rows + other % rows < one // steps_rows * rows + one % rows)
        & (other % steps_rows < rows)
    ).astype(f32).astype(bf16)
    order = jnp.dot(earlier, held.astype(bf16), preferred_element_type=f32)
    row = iota((count, LANES), 0)
    lane = iota((count, LANES), 1)
    slots = AT_ONCE * steps
    wanted = turn_ref[0] * AT_ONCE + lane // steps
    place = (
        (held > 0.0)
        & (order == wanted.astype(f32))
        & (row % steps_rows // rows == lane % steps)
        & (lane < slots)
    ).astype(f32).astype(bf16)
    place_ref[...] = place
    count_ref[0] = jnp.sum(
        jnp.where((row % steps_rows < rows) & (lane == 0), held, 0.0)
    ).astype(jnp.int32)
    down = (((0,), (0,)), ((), ()))
    x = lax.dot_general(place[:, :slots], x, down, preferred_element_type=f32).astype(bf16)
    page = lax.dot_general(place[:, :slots], data[:, width:], down, preferred_element_type=f32)
    chosen_ref[...] = page
    at_once = 256 // rank
    accum = jnp.zeros((slots, at_once * rank), f32)
    for first, block in page_blocks(page_refs, at_once):
        product = lax.dot_general(x, block, (((1,), (1,)), ((), ())), preferred_element_type=f32)
        accum = accum + jnp.where(page_columns(page, first, rank, at_once * rank), product, 0.0)
    folded = accum[:, :LANES] + accum[:, LANES:]
    folded = folded + pltpu.roll(folded, rank, 1)
    half = slots // 2
    packed = jnp.where(iota((half, LANES), 1) < rank, folded[:half], folded[half:]).astype(bf16)
    out_ref[...] = packed
    send_all(out_ref, out_hbm, sent)


def expand_kernel(part_ref, place_ref, chosen_ref, *refs):
    page_refs, out_ref = refs[:-1], refs[-1]
    members, steps_rows, width = out_ref.shape
    rank = page_refs[0].shape[1]
    slots = chosen_ref.shape[0]
    page = chosen_ref[...]
    packed = part_ref[0].astype(f32)
    for t in range(1, part_ref.shape[0]):
        packed = packed + part_ref[t].astype(f32)
    swapped = pltpu.roll(packed, rank, 1)
    left = iota(packed.shape, 1) < rank
    low = jnp.concatenate(
        [jnp.where(left, packed, swapped), jnp.where(left, swapped, packed)], axis=0
    )
    low = jnp.concatenate([low, low], axis=1).astype(bf16).astype(f32)
    at_once = 256 // rank
    accum = jnp.zeros((slots, width), f32)
    for first, block in page_blocks(page_refs, at_once):
        used = jnp.where(page_columns(page, first, rank, at_once * rank), low, 0.0)
        accum = accum + jnp.dot(used.astype(bf16), block, preferred_element_type=f32)
    result = (accum * ADAPTER_SCALE).astype(bf16)
    spread = jnp.dot(place_ref[:, :slots], result, preferred_element_type=f32).astype(bf16)
    out_ref[...] = spread.reshape(members, steps_rows, width)


def gather_kernel(part_ref, out_ref):
    steps, rows, _ = out_ref.shape
    total = part_ref[0].astype(f32)
    for z in range(1, part_ref.shape[0]):
        total = total + part_ref[z].astype(f32)
    for s in range(steps):
        out_ref[s] = total[s * rows : (s + 1) * rows].astype(bf16)


def per_device(
    queries, new_entries, cache, lengths, adapter_pages, request_slots, source_replica, source_slot
):
    replicas, tensors = lax.axis_size("replica"), lax.axis_size("tensor")
    z_size = replicas // X_SIZE
    groups = [[z * X_SIZE + x for z in range(z_size)] for x in range(X_SIZE)]
    members = len(groups[0])
    steps, rows, model = queries.shape
    width = model // tensors
    kv_heads = cache.shape[1]
    rank = adapter_pages.shape[2]
    sr = steps * rows
    count = members * sr

    def exchange(array, distance):
        return lax.ppermute(array, "replica", [(i, i ^ distance) for i in range(replicas)])

    shrink_own, expand_own = adapter_pages[:, 0], adapter_pages[:, 1]
    shrink_pages = [shrink_own] + [exchange(shrink_own, d) for d in BLOCK[1:]]
    expand_pages = [expand_own] + [exchange(expand_own, d) for d in BLOCK[1:]]

    parts = pl.pallas_call(
        attention_kernel,
        out_shape=pltpu.HBM((tensors, sr, width + LANES), bf16),
        in_specs=[hbm_spec()] * 4,
        out_specs=hbm_spec(),
        scratch_shapes=[
            pltpu.SMEM(lengths.shape, lengths.dtype),
            pltpu.VMEM(queries.shape, bf16),
            pltpu.VMEM(new_entries.shape, bf16),
            pltpu.VMEM((kv_heads,) + cache.shape[:1] + cache.shape[2:], bf16),
            pltpu.VMEM((sr, model), f32),
            pltpu.VMEM((tensors, sr, width + LANES), bf16),
            pltpu.SemaphoreType.DMA((3 + kv_heads,)),
            pltpu.SemaphoreType.DMA((kv_heads,)),
        ],
        compiler_params=params(),
        name="attention_part",
    )(*[in_hbm(array) for array in (lengths, queries, new_entries, cache)])
    parts = lax.all_to_all(parts, "tensor", 0, 0, tiled=True)

    attended, outgoing = pl.pallas_call(
        combine_kernel,
        out_shape=(
            jax.ShapeDtypeStruct((steps, rows, width), bf16),
            pltpu.HBM((members, sr, width + LANES), bf16),
        ),
        in_specs=[smem_spec(), smem_spec(), smem_spec(), vmem_spec()],
        out_specs=(vmem_spec(), hbm_spec()),
        scratch_shapes=[
            pltpu.VMEM((sr, width + LANES), bf16),
            pltpu.SemaphoreType.DMA((members,)),
        ],
        compiler_params=params(),
        name="combine",
    )(request_slots, source_replica[:, 0], source_slot, parts)
    column = lax.all_to_all(
        outgoing, "replica", 0, 0, tiled=True, axis_index_groups=groups
    )

    slots = AT_ONCE * steps

    def turn(k):
        low, place, chosen, held = pl.pallas_call(
            shrink_kernel,
            out_shape=(
                pltpu.HBM((tensors, slots // 2, LANES), bf16),
                jax.ShapeDtypeStruct((count, LANES), bf16),
                jax.ShapeDtypeStruct((slots, LANES), f32),
                jax.ShapeDtypeStruct((1,), jnp.int32),
            ),
            in_specs=[smem_spec()] + [vmem_spec()] * (1 + len(BLOCK)),
            out_specs=(hbm_spec(), vmem_spec(), vmem_spec(), smem_spec()),
            scratch_shapes=[
                pltpu.VMEM((slots // 2, LANES), bf16),
                pltpu.SemaphoreType.DMA((tensors,)),
            ],
            compiler_params=params(),
            name="shrink_part",
        )(jnp.full((1,), k, jnp.int32), column, *shrink_pages)
        low = lax.all_to_all(low, "tensor", 0, 0, tiled=True)
        back = pl.pallas_call(
            expand_kernel,
            out_shape=jax.ShapeDtypeStruct((members, sr, width), bf16),
            in_specs=[vmem_spec()] * (3 + len(BLOCK)),
            out_specs=vmem_spec(),
            compiler_params=params(),
            name="expand_rows",
        )(low, place, chosen, *expand_pages)
        return back, held[0]

    back, held = turn(0)
    _, back = lax.while_loop(
        lambda state: state[0] * AT_ONCE < held,
        lambda state: (state[0] + 1, state[1] + turn(state[0])[0]),
        (jnp.int32(1), back),
    )
    back = lax.all_to_all(back, "replica", 0, 0, tiled=True, axis_index_groups=groups)

    adapted = pl.pallas_call(
        gather_kernel,
        out_shape=jax.ShapeDtypeStruct((steps, rows, width), bf16),
        in_specs=[vmem_spec()],
        out_specs=vmem_spec(),
        compiler_params=params(),
        name="returned_rows",
    )(back)
    return attended, adapted


def solution(mesh):
    return jax.shard_map(
        per_device,
        mesh=mesh,
        in_specs=(
            P(None, "replica", None),
            P(None, "replica", None, None),
            P("replica", None, "tensor", None),
            P("replica"),
            P("replica", None, None, "tensor"),
            P("replica"),
            P("replica", None),
            P("replica"),
        ),
        out_specs=(P(None, "replica", "tensor"), P(None, "replica", "tensor")),
        check_vma=False,
    )
```

```python
import jax
import jax.numpy as jnp
from jax import lax
from jax.experimental import pallas as pl
from jax.experimental.pallas import tpu as pltpu
from jax.sharding import PartitionSpec as P

f32 = jnp.float32
bf16 = jnp.bfloat16

X_SIZE = 4
SLOTS = 8
ADAPTER_SCALE = 0.5
NEG_LARGE = -1e30
LANES = 128
LOG2_E = 1.4426950408889634
HELD = (0, 1, 3, X_SIZE)
ROWS = 4
AT_ONCE = 16


def vmem_spec():
    return pl.BlockSpec(memory_space=pltpu.VMEM)


def hbm_spec():
    return pl.BlockSpec(memory_space=pltpu.HBM)


def in_hbm(array):
    return pltpu.with_memory_space_constraint(array, pltpu.HBM)


def smem_spec():
    return pl.BlockSpec(memory_space=pltpu.SMEM)


def params():
    return pltpu.CompilerParams(vmem_limit_bytes=8 * 1024 * 1024)


def iota(shape, axis):
    return lax.broadcasted_iota(jnp.int32, shape, axis)


def attention_kernel(
    lengths_hbm,
    q_hbm,
    new_hbm,
    cache_hbm,
    out_hbm,
    lengths_ref,
    q_ref,
    new_ref,
    cache_ref,
    q_rows,
    out_ref,
    arrived,
    sent,
):
    copies = [
        pltpu.make_async_copy(q_hbm, q_ref, arrived.at[0]),
        pltpu.make_async_copy(new_hbm, new_ref, arrived.at[1]),
        pltpu.make_async_copy(lengths_hbm, lengths_ref, arrived.at[2]),
    ]
    cache_copies = [
        pltpu.make_async_copy(cache_hbm.at[:, g], cache_ref.at[g], arrived.at[3 + g])
        for g in range(cache_ref.shape[0])
    ]
    for copy in copies + cache_copies:
        copy.start()
    steps, rows, width = q_ref.shape
    kv_heads, local = cache_ref.shape[0], cache_ref.shape[2]
    head = cache_ref.shape[3] // 2
    group = width // head // kv_heads
    tensor_here = lax.axis_index("tensor")
    sr = steps * rows
    count = group * sr
    shape = (count, rows * local)
    row_id, col_id = iota(shape, 0), iota(shape, 1)
    request, col_request = row_id % rows, col_id // local
    fresh_shape = (count, steps * rows * kv_heads)
    fresh_row, fresh_col = iota(fresh_shape, 0), iota(fresh_shape, 1)
    fresh = (
        (fresh_row % rows == (fresh_col // kv_heads) % rows)
        & (fresh_col // (kv_heads * rows) <= (fresh_row // rows) % steps)
        & (tensor_here == 0)
    )
    fresh_head = jnp.where(fresh, fresh_col % kv_heads, -1)
    lane = iota((sr, LANES), 1)
    per_tile = out_ref.shape[2] // head - 1
    field = LANES // 2 // per_tile
    factor = head ** (-0.5) * LOG2_E
    contract = (((1,), (1,)), ((), ()))
    for copy in copies + cache_copies:
        copy.wait()
    length = jnp.zeros(shape, jnp.int32)
    for r in range(rows):
        length = jnp.where(col_request == r, lengths_ref[r], length)
    visible = (request == col_request) & (tensor_here * local + col_id % local < length)
    for s in range(steps):
        q_rows[s * rows : (s + 1) * rows, :] = q_ref[s].astype(f32)
    new_all = new_ref[...].astype(f32).reshape(steps * rows * kv_heads, 2 * head).astype(bf16)
    new_keys, new_values = new_all[:, :head], new_all[:, head:]
    ones = jnp.ones((rows * local + new_keys.shape[0], head), bf16)
    out_copies = []
    for g in range(kv_heads):
        q = jnp.concatenate(
            [q_rows[:, (g * group + k) * head : (g * group + k + 1) * head] for k in range(group)],
            axis=0,
        ).astype(bf16)
        keys = cache_ref[g, :, :, :head].reshape(rows * local, head)
        values = cache_ref[g, :, :, head:].reshape(rows * local, head)
        keys = jnp.concatenate([keys, new_keys], axis=0)
        values = jnp.concatenate([values, new_values], axis=0)
        values = jnp.concatenate([values, ones], axis=1)
        scores = lax.dot_general(q, keys, contract, preferred_element_type=f32) * factor
        old_scores = jnp.where(visible, scores[:, : rows * local], NEG_LARGE)
        new_scores = jnp.where(fresh_head == g, scores[:, rows * local :], NEG_LARGE)
        top = jnp.max(jnp.maximum(old_scores, new_scores), axis=1, keepdims=True)
        shift = jnp.maximum(top, 0.01 * NEG_LARGE).astype(bf16).astype(f32)
        weights = jnp.concatenate(
            [jnp.exp2(old_scores - shift), jnp.exp2(new_scores - shift)], axis=1
        ).astype(bf16)
        sums = jnp.dot(weights, values, preferred_element_type=f32)
        accum, total = sums[:, :head], sums[:, head:]
        for first in range(0, group, per_tile):
            place = (g * group + first) // per_tile
            stats = jnp.zeros((sr, LANES), f32)
            for k in range(per_tile):
                part = slice((first + k) * sr, (first + k + 1) * sr)
                out_ref[place, :, k * head : (k + 1) * head] = accum[part].astype(bf16)
                stats = jnp.where(lane // field == k, shift[part], stats)
                stats = jnp.where(lane // field == per_tile + k, total[part], stats)
            out_ref[place, :, per_tile * head :] = stats.astype(bf16)
        places = group // per_tile
        here = pl.ds(g * places, places)
        out_copies.append(
            pltpu.make_async_copy(out_ref.at[here], out_hbm.at[here], sent.at[g])
        )
        out_copies[-1].start()
    for copy in out_copies:
        copy.wait()


def send_all(ref, hbm, sent):
    copies = [
        pltpu.make_async_copy(ref, hbm.at[i], sent.at[i]) for i in range(hbm.shape[0])
    ]
    for copy in copies:
        copy.start()
    for copy in copies:
        copy.wait()


def combine_kernel(slots_ref, source_ref, source_slot_ref, part_ref, attended_ref, send_hbm, send_ref, sent):
    steps, rows, width = attended_ref.shape
    sources = part_ref.shape[0]
    per_tile = width // LANES
    field = LANES // 2 // per_tile
    stats = [part_ref[t, :, width:].astype(f32) for t in range(sources)]
    top = stats[0]
    for t in range(1, sources):
        top = jnp.maximum(top, stats[t])
    sums = [jnp.zeros((steps * rows, LANES), f32) for _ in range(per_tile)]
    total = jnp.zeros((steps * rows, LANES), f32)
    for t in range(sources):
        fade = jnp.exp2(stats[t] - top)
        total = total + fade * pltpu.roll(stats[t], LANES // 2, 1)
        for k in range(per_tile):
            sums[k] = sums[k] + fade[:, k * field : k * field + 1] * part_ref[
                t, :, k * LANES : (k + 1) * LANES
            ].astype(f32)
    replica_here = lax.axis_index("replica")
    row = iota((steps * rows, LANES), 0) % rows
    page = jnp.zeros((steps * rows, LANES), f32)
    for r in range(rows):
        slot = slots_ref[r]
        entry = jnp.clip(slot - SLOTS, 0, source_slot_ref.shape[0] - 1)
        number = jnp.where(
            slot < SLOTS,
            replica_here * SLOTS + slot,
            source_ref[entry] * SLOTS + source_slot_ref[entry],
        )
        page = jnp.where(row == r, number.astype(f32), page)
    page = page.astype(bf16)
    for k in range(per_tile):
        attended = sums[k] / total[:, k * field : k * field + 1]
        for s in range(steps):
            attended_ref[s, :, k * LANES : (k + 1) * LANES] = attended[
                s * rows : (s + 1) * rows
            ].astype(bf16)
        rounded = attended.astype(bf16)
        send_ref[:, k * LANES : (k + 1) * LANES] = rounded
    send_ref[:, width:] = page
    send_all(send_ref, send_hbm, sent)


def page_columns(page, first, rank, width):
    return page[:, :1] == (first + iota((page.shape[0], width), 1) // rank).astype(f32)


def page_blocks(refs, at_once):
    replica_here = lax.axis_index("replica")
    for distance, ref in zip(HELD, refs):
        first = jnp.bitwise_xor(replica_here, distance) * SLOTS
        for p in range(0, ref.shape[0], at_once):
            block = ref[p : p + at_once]
            yield first + p, block.reshape(at_once * block.shape[1], block.shape[2])


def shrink_kernel(
    turn_ref,
    rows_ref,
    *refs,
):
    members, steps_rows, padded = rows_ref.shape
    page_refs = refs[: len(HELD)]
    out_hbm, place_ref, chosen_ref, count_ref, out_ref, sent = refs[len(HELD) :]
    rank, width = page_refs[0].shape[1:]
    count = members * steps_rows
    rows = ROWS
    steps = steps_rows // rows
    data = rows_ref[...].reshape(count, padded)
    x, page = data[:, :width], data[:, width:].astype(f32)
    distance = jnp.bitwise_xor(page.astype(jnp.int32) // SLOTS, lax.axis_index("replica"))
    held = distance == HELD[0]
    for other in HELD[1:]:
        held = held | (distance == other)
    held = held.astype(f32)
    one, other = iota((count, count), 0), iota((count, count), 1)
    earlier = (
        (other // steps_rows * rows + other % rows < one // steps_rows * rows + one % rows)
        & (other % steps_rows < rows)
    ).astype(f32).astype(bf16)
    order = jnp.dot(earlier, held.astype(bf16), preferred_element_type=f32)
    row = iota((count, LANES), 0)
    lane = iota((count, LANES), 1)
    slots = AT_ONCE * steps
    wanted = turn_ref[0] * AT_ONCE + lane // steps
    place = (
        (held > 0.0)
        & (order == wanted.astype(f32))
        & (row % steps_rows // rows == lane % steps)
        & (lane < slots)
    ).astype(f32).astype(bf16)
    place_ref[...] = place
    count_ref[0] = jnp.sum(
        jnp.where((row % steps_rows < rows) & (lane == 0), held, 0.0)
    ).astype(jnp.int32)
    down = (((0,), (0,)), ((), ()))
    x = lax.dot_general(place[:, :slots], x, down, preferred_element_type=f32).astype(bf16)
    page = lax.dot_general(place[:, :slots], data[:, width:], down, preferred_element_type=f32)
    chosen_ref[...] = page
    at_once = 256 // rank
    accum = jnp.zeros((slots, at_once * rank), f32)
    for first, block in page_blocks(page_refs, at_once):
        product = lax.dot_general(x, block, (((1,), (1,)), ((), ())), preferred_element_type=f32)
        accum = accum + jnp.where(page_columns(page, first, rank, at_once * rank), product, 0.0)
    folded = accum[:, :LANES] + accum[:, LANES:]
    folded = folded + pltpu.roll(folded, rank, 1)
    half = slots // 2
    packed = jnp.where(iota((half, LANES), 1) < rank, folded[:half], folded[half:]).astype(bf16)
    out_ref[...] = packed
    send_all(out_ref, out_hbm, sent)


def expand_kernel(part_ref, place_ref, chosen_ref, *refs):
    page_refs, out_ref = refs[:-1], refs[-1]
    members, steps_rows, width = out_ref.shape
    rank = page_refs[0].shape[1]
    slots = chosen_ref.shape[0]
    page = chosen_ref[...]
    packed = part_ref[0].astype(f32)
    for t in range(1, part_ref.shape[0]):
        packed = packed + part_ref[t].astype(f32)
    swapped = pltpu.roll(packed, rank, 1)
    left = iota(packed.shape, 1) < rank
    low = jnp.concatenate(
        [jnp.where(left, packed, swapped), jnp.where(left, swapped, packed)], axis=0
    )
    low = jnp.concatenate([low, low], axis=1).astype(bf16).astype(f32)
    at_once = 256 // rank
    accum = jnp.zeros((slots, width), f32)
    for first, block in page_blocks(page_refs, at_once):
        used = jnp.where(page_columns(page, first, rank, at_once * rank), low, 0.0)
        accum = accum + jnp.dot(used.astype(bf16), block, preferred_element_type=f32)
    result = (accum * ADAPTER_SCALE).astype(bf16)
    spread = jnp.dot(place_ref[:, :slots], result, preferred_element_type=f32).astype(bf16)
    out_ref[...] = spread.reshape(members, steps_rows, width)


def gather_kernel(part_ref, out_ref):
    steps, rows, _ = out_ref.shape
    total = part_ref[0].astype(f32)
    for z in range(1, part_ref.shape[0]):
        total = total + part_ref[z].astype(f32)
    for s in range(steps):
        out_ref[s] = total[s * rows : (s + 1) * rows].astype(bf16)


def per_device(
    queries, new_entries, cache, lengths, adapter_pages, request_slots, source_replica, source_slot
):
    replicas, tensors = lax.axis_size("replica"), lax.axis_size("tensor")
    z_size = replicas // X_SIZE
    groups = [
        [z * X_SIZE + (x ^ (z % 2 * X_SIZE // 2)) for z in range(z_size)] for x in range(X_SIZE)
    ]
    members = len(groups[0])
    steps, rows, model = queries.shape
    width = model // tensors
    kv_heads = cache.shape[1]
    rank = adapter_pages.shape[2]
    sr = steps * rows
    count = members * sr

    def exchange(array, distance):
        return lax.ppermute(array, "replica", [(i, i ^ distance) for i in range(replicas)])

    shrink_own, expand_own = adapter_pages[:, 0], adapter_pages[:, 1]
    shrink_pages = [shrink_own] + [exchange(shrink_own, d) for d in HELD[1:]]
    expand_pages = [expand_own] + [exchange(expand_own, d) for d in HELD[1:]]

    parts = pl.pallas_call(
        attention_kernel,
        out_shape=pltpu.HBM((tensors, sr, width + LANES), bf16),
        in_specs=[hbm_spec()] * 4,
        out_specs=hbm_spec(),
        scratch_shapes=[
            pltpu.SMEM(lengths.shape, lengths.dtype),
            pltpu.VMEM(queries.shape, bf16),
            pltpu.VMEM(new_entries.shape, bf16),
            pltpu.VMEM((kv_heads,) + cache.shape[:1] + cache.shape[2:], bf16),
            pltpu.VMEM((sr, model), f32),
            pltpu.VMEM((tensors, sr, width + LANES), bf16),
            pltpu.SemaphoreType.DMA((3 + kv_heads,)),
            pltpu.SemaphoreType.DMA((kv_heads,)),
        ],
        compiler_params=params(),
        name="attention_part",
    )(*[in_hbm(array) for array in (lengths, queries, new_entries, cache)])
    parts = lax.all_to_all(parts, "tensor", 0, 0, tiled=True)

    attended, outgoing = pl.pallas_call(
        combine_kernel,
        out_shape=(
            jax.ShapeDtypeStruct((steps, rows, width), bf16),
            pltpu.HBM((members, sr, width + LANES), bf16),
        ),
        in_specs=[smem_spec(), smem_spec(), smem_spec(), vmem_spec()],
        out_specs=(vmem_spec(), hbm_spec()),
        scratch_shapes=[
            pltpu.VMEM((sr, width + LANES), bf16),
            pltpu.SemaphoreType.DMA((members,)),
        ],
        compiler_params=params(),
        name="combine",
    )(request_slots, source_replica[:, 0], source_slot, parts)
    column = lax.all_to_all(
        outgoing, "replica", 0, 0, tiled=True, axis_index_groups=groups
    )

    slots = AT_ONCE * steps

    def turn(k):
        low, place, chosen, held = pl.pallas_call(
            shrink_kernel,
            out_shape=(
                pltpu.HBM((tensors, slots // 2, LANES), bf16),
                jax.ShapeDtypeStruct((count, LANES), bf16),
                jax.ShapeDtypeStruct((slots, LANES), f32),
                jax.ShapeDtypeStruct((1,), jnp.int32),
            ),
            in_specs=[smem_spec()] + [vmem_spec()] * (1 + len(HELD)),
            out_specs=(hbm_spec(), vmem_spec(), vmem_spec(), smem_spec()),
            scratch_shapes=[
                pltpu.VMEM((slots // 2, LANES), bf16),
                pltpu.SemaphoreType.DMA((tensors,)),
            ],
            compiler_params=params(),
            name="shrink_part",
        )(jnp.full((1,), k, jnp.int32), column, *shrink_pages)
        low = lax.all_to_all(low, "tensor", 0, 0, tiled=True)
        back = pl.pallas_call(
            expand_kernel,
            out_shape=pltpu.VMEM((members, sr, width), bf16),
            in_specs=[vmem_spec()] * (3 + len(HELD)),
            out_specs=vmem_spec(),
            compiler_params=params(),
            name="expand_rows",
        )(low, place, chosen, *expand_pages)
        return back, held[0]

    back, held = turn(0)
    _, back = lax.while_loop(
        lambda state: state[0] * AT_ONCE < held,
        lambda state: (state[0] + 1, state[1] + turn(state[0])[0]),
        (jnp.int32(1), back),
    )
    back = lax.all_to_all(back, "replica", 0, 0, tiled=True, axis_index_groups=groups)

    adapted = pl.pallas_call(
        gather_kernel,
        out_shape=jax.ShapeDtypeStruct((steps, rows, width), bf16),
        in_specs=[vmem_spec()],
        out_specs=vmem_spec(),
        compiler_params=params(),
        name="returned_rows",
    )(back)
    return attended, adapted


def solution(mesh):
    return jax.shard_map(
        per_device,
        mesh=mesh,
        in_specs=(
            P(None, "replica", None),
            P(None, "replica", None, None),
            P("replica", None, "tensor", None),
            P("replica"),
            P("replica", None, None, "tensor"),
            P("replica"),
            P("replica", None),
            P("replica"),
        ),
        out_specs=(P(None, "replica", "tensor"), P(None, "replica", "tensor")),
        check_vma=False,
    )
```

```python
import jax
import jax.numpy as jnp
from jax import lax
from jax.experimental import pallas as pl
from jax.experimental.pallas import tpu as pltpu
from jax.sharding import PartitionSpec as P

f32 = jnp.float32
bf16 = jnp.bfloat16

X_SIZE = 4
SLOTS = 8
ADAPTER_SCALE = 0.5
NEG_LARGE = -1e30
LANES = 128
LOG2_E = 1.4426950408889634
HELD = (0, 1, 3, X_SIZE)
ROWS = 4
AT_ONCE = 16


def vmem_spec():
    return pl.BlockSpec(memory_space=pltpu.VMEM)


def hbm_spec():
    return pl.BlockSpec(memory_space=pltpu.HBM)


def in_hbm(array):
    return pltpu.with_memory_space_constraint(array, pltpu.HBM)


def smem_spec():
    return pl.BlockSpec(memory_space=pltpu.SMEM)


def params():
    return pltpu.CompilerParams(vmem_limit_bytes=8 * 1024 * 1024)


def iota(shape, axis):
    return lax.broadcasted_iota(jnp.int32, shape, axis)


def attention_kernel(
    lengths_hbm,
    q_hbm,
    new_hbm,
    cache_hbm,
    slots_hbm,
    source_hbm,
    source_slot_hbm,
    out_hbm,
    page_ref,
    lengths_ref,
    slots_ref,
    source_ref,
    source_slot_ref,
    q_ref,
    new_ref,
    cache_ref,
    q_rows,
    out_ref,
    arrived,
    sent,
    planned,
):
    copies = [
        pltpu.make_async_copy(q_hbm, q_ref, arrived.at[0]),
        pltpu.make_async_copy(new_hbm, new_ref, arrived.at[1]),
        pltpu.make_async_copy(lengths_hbm, lengths_ref, arrived.at[2]),
    ]
    plan_copies = [
        pltpu.make_async_copy(slots_hbm, slots_ref, planned.at[0]),
        pltpu.make_async_copy(source_hbm, source_ref, planned.at[1]),
        pltpu.make_async_copy(source_slot_hbm, source_slot_ref, planned.at[2]),
    ]
    cache_copies = [
        pltpu.make_async_copy(cache_hbm.at[:, g], cache_ref.at[g], arrived.at[3 + g])
        for g in range(cache_ref.shape[0])
    ]
    for copy in copies + cache_copies + plan_copies:
        copy.start()
    steps, rows, width = q_ref.shape
    kv_heads, local = cache_ref.shape[0], cache_ref.shape[2]
    head = cache_ref.shape[3] // 2
    group = width // head // kv_heads
    tensor_here = lax.axis_index("tensor")
    sr = steps * rows
    count = group * sr
    shape = (count, rows * local)
    row_id, col_id = iota(shape, 0), iota(shape, 1)
    request, col_request = row_id % rows, col_id // local
    fresh_shape = (count, steps * rows * kv_heads)
    fresh_row, fresh_col = iota(fresh_shape, 0), iota(fresh_shape, 1)
    fresh = (
        (fresh_row % rows == (fresh_col // kv_heads) % rows)
        & (fresh_col // (kv_heads * rows) <= (fresh_row // rows) % steps)
        & (tensor_here == 0)
    )
    fresh_head = jnp.where(fresh, fresh_col % kv_heads, -1)
    lane = iota((sr, LANES), 1)
    per_tile = out_ref.shape[2] // head - 1
    field = LANES // 2 // per_tile
    factor = head ** (-0.5) * LOG2_E
    contract = (((1,), (1,)), ((), ()))
    for copy in copies + cache_copies:
        copy.wait()
    length = jnp.zeros(shape, jnp.int32)
    for r in range(rows):
        length = jnp.where(col_request == r, lengths_ref[r], length)
    visible = (request == col_request) & (tensor_here * local + col_id % local < length)
    for s in range(steps):
        q_rows[s * rows : (s + 1) * rows, :] = q_ref[s].astype(f32)
    new_all = new_ref[...].astype(f32).reshape(steps * rows * kv_heads, 2 * head).astype(bf16)
    new_keys, new_values = new_all[:, :head], new_all[:, head:]
    ones = jnp.ones((rows * local + new_keys.shape[0], head), bf16)
    out_copies = []
    for g in range(kv_heads):
        q = jnp.concatenate(
            [q_rows[:, (g * group + k) * head : (g * group + k + 1) * head] for k in range(group)],
            axis=0,
        ).astype(bf16)
        keys = cache_ref[g, :, :, :head].reshape(rows * local, head)
        values = cache_ref[g, :, :, head:].reshape(rows * local, head)
        keys = jnp.concatenate([keys, new_keys], axis=0)
        values = jnp.concatenate([values, new_values], axis=0)
        values = jnp.concatenate([values, ones], axis=1)
        scores = lax.dot_general(q, keys, contract, preferred_element_type=f32) * factor
        old_scores = jnp.where(visible, scores[:, : rows * local], NEG_LARGE)
        new_scores = jnp.where(fresh_head == g, scores[:, rows * local :], NEG_LARGE)
        top = jnp.max(jnp.maximum(old_scores, new_scores), axis=1, keepdims=True)
        shift = jnp.maximum(top, 0.01 * NEG_LARGE).astype(bf16).astype(f32)
        weights = jnp.concatenate(
            [jnp.exp2(old_scores - shift), jnp.exp2(new_scores - shift)], axis=1
        ).astype(bf16)
        sums = jnp.dot(weights, values, preferred_element_type=f32)
        accum, total = sums[:, :head], sums[:, head:]
        for first in range(0, group, per_tile):
            place = (g * group + first) // per_tile
            stats = jnp.zeros((sr, LANES), f32)
            for k in range(per_tile):
                part = slice((first + k) * sr, (first + k + 1) * sr)
                out_ref[place, :, k * head : (k + 1) * head] = accum[part].astype(bf16)
                stats = jnp.where(lane // field == k, shift[part], stats)
                stats = jnp.where(lane // field == per_tile + k, total[part], stats)
            out_ref[place, :, per_tile * head :] = stats.astype(bf16)
        places = group // per_tile
        here = pl.ds(g * places, places)
        out_copies.append(
            pltpu.make_async_copy(out_ref.at[here], out_hbm.at[here], sent.at[g])
        )
        out_copies[-1].start()
    for copy in plan_copies:
        copy.wait()
    replica_here = lax.axis_index("replica")
    row = iota((steps * rows, LANES), 0) % rows
    page = jnp.zeros((steps * rows, LANES), f32)
    for r in range(rows):
        slot = slots_ref[r]
        entry = jnp.clip(slot - SLOTS, 0, source_slot_ref.shape[0] - 1)
        number = jnp.where(
            slot < SLOTS,
            replica_here * SLOTS + slot,
            source_ref[entry] * SLOTS + source_slot_ref[entry],
        )
        page = jnp.where(row == r, number.astype(f32), page)
    page_ref[...] = page.astype(bf16)
    for copy in out_copies:
        copy.wait()


def send_all(ref, hbm, sent):
    copies = [
        pltpu.make_async_copy(ref, hbm.at[i], sent.at[i]) for i in range(hbm.shape[0])
    ]
    for copy in copies:
        copy.start()
    for copy in copies:
        copy.wait()


def combine_kernel(page_ref, part_ref, attended_ref, send_hbm, send_ref, sent):
    steps, rows, width = attended_ref.shape
    sources = part_ref.shape[0]
    per_tile = width // LANES
    field = LANES // 2 // per_tile
    sr = steps * rows
    stats = part_ref[:, :, width:].astype(f32)
    top = stats[0]
    for t in range(1, sources):
        top = jnp.maximum(top, stats[t])
    fade = jnp.exp2(stats - top[None]).astype(bf16).reshape(sources * sr, LANES)
    lane, column = iota((LANES, width), 0), iota((LANES, width), 1) // LANES * field
    spread = lax.dot(fade, (lane == column).astype(f32).astype(bf16), preferred_element_type=f32)
    totals = lax.dot(
        part_ref[:, :, width:].reshape(sources * sr, LANES),
        (lane == column + LANES // 2).astype(f32).astype(bf16),
        preferred_element_type=f32,
    )
    sums = jnp.zeros((sr, width), f32)
    total = jnp.zeros((sr, width), f32)
    for t in range(sources):
        part = slice(t * sr, (t + 1) * sr)
        sums = sums + spread[part] * part_ref[t, :, :width].astype(f32)
        total = total + spread[part] * totals[part]
    attended_all = sums / total
    for k in range(per_tile):
        attended = attended_all[:, k * LANES : (k + 1) * LANES]
        for s in range(steps):
            attended_ref[s, :, k * LANES : (k + 1) * LANES] = attended[
                s * rows : (s + 1) * rows
            ].astype(bf16)
        rounded = attended.astype(bf16)
        send_ref[:, k * LANES : (k + 1) * LANES] = rounded
    send_ref[:, width:] = page_ref[...]
    send_all(send_ref, send_hbm, sent)


def page_columns(page, first, rank, width):
    return page[:, :1] == (first + iota((page.shape[0], width), 1) // rank).astype(f32)


def page_blocks(refs, at_once):
    replica_here = lax.axis_index("replica")
    for distance, ref in zip(HELD, refs):
        first = jnp.bitwise_xor(replica_here, distance) * SLOTS
        for p in range(0, ref.shape[0], at_once):
            block = ref[p : p + at_once]
            yield first + p, block.reshape(at_once * block.shape[1], block.shape[2])


def shrink_kernel(rows_ref, *refs):
    members, steps_rows, padded = rows_ref.shape
    page_refs = refs[: len(HELD)]
    turn_refs = refs[len(HELD) : -5]
    out_hbm, place_ref, chosen_ref, out_ref, sent = refs[-5:]
    turn = turn_refs[0][0] if turn_refs else 0
    rank, width = page_refs[0].shape[1:]
    count = members * steps_rows
    rows = ROWS
    steps = steps_rows // rows
    data = rows_ref[...].reshape(count, padded)
    x, page = data[:, :width], data[:, width:].astype(f32)
    distance = jnp.bitwise_xor(page.astype(jnp.int32) // SLOTS, lax.axis_index("replica"))
    held = distance == HELD[0]
    for other in HELD[1:]:
        held = held | (distance == other)
    held = held.astype(f32)
    one, other = iota((count, count), 0), iota((count, count), 1)
    earlier = (
        (other // steps_rows * rows + other % rows < one // steps_rows * rows + one % rows)
        & (other % steps_rows < rows)
    ).astype(f32).astype(bf16)
    order = jnp.dot(earlier, held.astype(bf16), preferred_element_type=f32)
    row = iota((count, LANES), 0)
    lane = iota((count, LANES), 1)
    slots = AT_ONCE * steps
    wanted = turn * AT_ONCE + lane // steps
    place = (
        (held > 0.0)
        & (order == wanted.astype(f32))
        & (row % steps_rows // rows == lane % steps)
        & (lane < slots)
    ).astype(f32).astype(bf16)
    place_ref[...] = place
    at_once = 256 // rank
    accum = jnp.zeros((count, at_once * rank), f32)
    for first, block in page_blocks(page_refs, at_once):
        product = lax.dot_general(x, block, (((1,), (1,)), ((), ())), preferred_element_type=f32)
        accum = accum + jnp.where(page_columns(page, first, rank, at_once * rank), product, 0.0)
    folded = accum[:, :LANES] + accum[:, LANES:]
    folded = (folded + pltpu.roll(folded, rank, 1)).astype(bf16)
    down = (((0,), (0,)), ((), ()))
    both = jnp.concatenate([folded, data[:, width:]], axis=1)
    both = lax.dot_general(place[:, :slots], both, down, preferred_element_type=f32)
    folded, chosen_ref[...] = both[:, :LANES], both[:, LANES:]
    half = slots // 2
    packed = jnp.where(iota((half, LANES), 1) < rank, folded[:half], folded[half:]).astype(bf16)
    out_ref[...] = packed
    send_all(out_ref, out_hbm, sent)


def expand_kernel(part_ref, place_ref, chosen_ref, *refs):
    page_refs, out_ref = refs[:-1], refs[-1]
    members, steps_rows, width = out_ref.shape
    rank = page_refs[0].shape[1]
    slots = chosen_ref.shape[0]
    page = chosen_ref[...]
    packed = part_ref[0].astype(f32)
    for t in range(1, part_ref.shape[0]):
        packed = packed + part_ref[t].astype(f32)
    swapped = pltpu.roll(packed, rank, 1)
    left = iota(packed.shape, 1) < rank
    low = jnp.concatenate(
        [jnp.where(left, packed, swapped), jnp.where(left, swapped, packed)], axis=0
    )
    low = jnp.concatenate([low, low], axis=1).astype(bf16).astype(f32)
    at_once = 256 // rank
    accum = jnp.zeros((slots, width), f32)
    for first, block in page_blocks(page_refs, at_once):
        used = jnp.where(page_columns(page, first, rank, at_once * rank), low, 0.0)
        accum = accum + jnp.dot(used.astype(bf16), block, preferred_element_type=f32)
    result = (accum * ADAPTER_SCALE).astype(bf16)
    spread = jnp.dot(place_ref[:, :slots], result, preferred_element_type=f32).astype(bf16)
    out_ref[...] = spread.reshape(members, steps_rows, width)


def gather_kernel(part_ref, out_ref):
    steps, rows, _ = out_ref.shape
    total = part_ref[0].astype(f32)
    for z in range(1, part_ref.shape[0]):
        total = total + part_ref[z].astype(f32)
    for s in range(steps):
        out_ref[s] = total[s * rows : (s + 1) * rows].astype(bf16)


def per_device(
    queries, new_entries, cache, lengths, adapter_pages, request_slots, source_replica, source_slot
):
    replicas, tensors = lax.axis_size("replica"), lax.axis_size("tensor")
    z_size = replicas // X_SIZE
    groups = [
        [z * X_SIZE + (x ^ (z % 2 * X_SIZE // 2)) for z in range(z_size)] for x in range(X_SIZE)
    ]
    members = len(groups[0])
    steps, rows, model = queries.shape
    width = model // tensors
    kv_heads = cache.shape[1]
    rank = adapter_pages.shape[2]
    sr = steps * rows
    count = members * sr

    def exchange(array, distance):
        return lax.ppermute(array, "replica", [(i, i ^ distance) for i in range(replicas)])

    shrink_own, expand_own = adapter_pages[:, 0], adapter_pages[:, 1]
    shrink_pages = [shrink_own] + [exchange(shrink_own, d) for d in HELD[1:]]
    expand_pages = [expand_own] + [exchange(expand_own, d) for d in HELD[1:]]

    plan = (request_slots, source_replica[:, 0], source_slot)
    parts, page = pl.pallas_call(
        attention_kernel,
        out_shape=(
            pltpu.HBM((tensors, sr, width + LANES), bf16),
            pltpu.VMEM((sr, LANES), bf16),
        ),
        in_specs=[hbm_spec()] * 7,
        out_specs=(hbm_spec(), vmem_spec()),
        scratch_shapes=[
            pltpu.SMEM(lengths.shape, lengths.dtype),
            *[pltpu.SMEM(array.shape, array.dtype) for array in plan],
            pltpu.VMEM(queries.shape, bf16),
            pltpu.VMEM(new_entries.shape, bf16),
            pltpu.VMEM((kv_heads,) + cache.shape[:1] + cache.shape[2:], bf16),
            pltpu.VMEM((sr, model), f32),
            pltpu.VMEM((tensors, sr, width + LANES), bf16),
            pltpu.SemaphoreType.DMA((3 + kv_heads,)),
            pltpu.SemaphoreType.DMA((kv_heads,)),
            pltpu.SemaphoreType.DMA((3,)),
        ],
        compiler_params=params(),
        name="attention_part",
    )(*[in_hbm(array) for array in (lengths, queries, new_entries, cache) + plan])
    parts = lax.all_to_all(parts, "tensor", 0, 0, tiled=True)

    attended, outgoing = pl.pallas_call(
        combine_kernel,
        out_shape=(
            jax.ShapeDtypeStruct((steps, rows, width), bf16),
            pltpu.HBM((members, sr, width + LANES), bf16),
        ),
        in_specs=[vmem_spec(), vmem_spec()],
        out_specs=(vmem_spec(), hbm_spec()),
        scratch_shapes=[
            pltpu.VMEM((sr, width + LANES), bf16),
            pltpu.SemaphoreType.DMA((members,)),
        ],
        compiler_params=params(),
        name="combine",
    )(page, parts)
    column = lax.all_to_all(
        outgoing, "replica", 0, 0, tiled=True, axis_index_groups=groups
    )

    slots = AT_ONCE * steps

    def turn(k):
        number = () if k is None else (jnp.full((1,), k, jnp.int32),)
        low, place, chosen = pl.pallas_call(
            shrink_kernel,
            out_shape=(
                pltpu.HBM((tensors, slots // 2, LANES), bf16),
                jax.ShapeDtypeStruct((count, LANES), bf16),
                jax.ShapeDtypeStruct((slots, LANES), f32),
            ),
            in_specs=[vmem_spec()] * (1 + len(HELD)) + [smem_spec()] * len(number),
            out_specs=(hbm_spec(), vmem_spec(), vmem_spec()),
            scratch_shapes=[
                pltpu.VMEM((slots // 2, LANES), bf16),
                pltpu.SemaphoreType.DMA((tensors,)),
            ],
            compiler_params=params(),
            name="shrink_part",
        )(column, *shrink_pages, *number)
        low = lax.all_to_all(low, "tensor", 0, 0, tiled=True)
        back = pl.pallas_call(
            expand_kernel,
            out_shape=pltpu.VMEM((members, sr, width), bf16),
            in_specs=[vmem_spec()] * (3 + len(HELD)),
            out_specs=vmem_spec(),
            compiler_params=params(),
            name="expand_rows",
        )(low, place, chosen, *expand_pages)
        return back

    back = turn(None)
    distance = (column[:, :rows, width].astype(f32).astype(jnp.int32) // SLOTS) ^ lax.axis_index(
        "replica"
    )
    held = sum(jnp.sum((distance == other).astype(jnp.int32)) for other in HELD)
    _, back = lax.while_loop(
        lambda state: state[0] * AT_ONCE < held,
        lambda state: (state[0] + 1, state[1] + turn(state[0])),
        (jnp.int32(1), back),
    )
    back = lax.all_to_all(back, "replica", 0, 0, tiled=True, axis_index_groups=groups)

    adapted = pl.pallas_call(
        gather_kernel,
        out_shape=jax.ShapeDtypeStruct((steps, rows, width), bf16),
        in_specs=[vmem_spec()],
        out_specs=vmem_spec(),
        compiler_params=params(),
        name="returned_rows",
    )(back)
    return attended, adapted


def solution(mesh):
    return jax.shard_map(
        per_device,
        mesh=mesh,
        in_specs=(
            P(None, "replica", None),
            P(None, "replica", None, None),
            P("replica", None, "tensor", None),
            P("replica"),
            P("replica", None, None, "tensor"),
            P("replica"),
            P("replica", None),
            P("replica"),
        ),
        out_specs=(P(None, "replica", "tensor"), P(None, "replica", "tensor")),
        check_vma=False,
    )
```

```python
import jax
import jax.numpy as jnp
from jax import lax
from jax.experimental import pallas as pl
from jax.experimental.pallas import tpu as pltpu
from jax.sharding import PartitionSpec as P

f32 = jnp.float32
bf16 = jnp.bfloat16

X_SIZE = 4
SLOTS = 8
ADAPTER_SCALE = 0.5
NEG_LARGE = -1e30
LANES = 128
LOG2_E = 1.4426950408889634
HELD = (0, 1, 3, X_SIZE)
ROWS = 4
AT_ONCE = 16


def vmem_spec():
    return pl.BlockSpec(memory_space=pltpu.VMEM)


def hbm_spec():
    return pl.BlockSpec(memory_space=pltpu.HBM)


def in_hbm(array):
    return pltpu.with_memory_space_constraint(array, pltpu.HBM)


def in_vmem(array):
    return pltpu.with_memory_space_constraint(array, pltpu.VMEM)


def smem_spec():
    return pl.BlockSpec(memory_space=pltpu.SMEM)


def params():
    return pltpu.CompilerParams(vmem_limit_bytes=8 * 1024 * 1024)


def iota(shape, axis):
    return lax.broadcasted_iota(jnp.int32, shape, axis)


def attention_kernel(
    lengths_hbm,
    q_hbm,
    new_hbm,
    cache_hbm,
    slots_hbm,
    source_hbm,
    source_slot_hbm,
    out_hbm,
    page_ref,
    lengths_ref,
    slots_ref,
    source_ref,
    source_slot_ref,
    q_ref,
    new_ref,
    cache_ref,
    q_rows,
    out_ref,
    arrived,
    sent,
    planned,
):
    copies = [
        pltpu.make_async_copy(q_hbm, q_ref, arrived.at[0]),
        pltpu.make_async_copy(new_hbm, new_ref, arrived.at[1]),
        pltpu.make_async_copy(lengths_hbm, lengths_ref, arrived.at[2]),
    ]
    plan_copies = [
        pltpu.make_async_copy(slots_hbm, slots_ref, planned.at[0]),
        pltpu.make_async_copy(source_hbm, source_ref, planned.at[1]),
        pltpu.make_async_copy(source_slot_hbm, source_slot_ref, planned.at[2]),
    ]
    cache_copies = [
        pltpu.make_async_copy(cache_hbm.at[:, g], cache_ref.at[g], arrived.at[3 + g])
        for g in range(cache_ref.shape[0])
    ]
    for copy in copies + cache_copies + plan_copies:
        copy.start()
    steps, rows, width = q_ref.shape
    kv_heads, local = cache_ref.shape[0], cache_ref.shape[2]
    head = cache_ref.shape[3] // 2
    group = width // head // kv_heads
    tensor_here = lax.axis_index("tensor")
    sr = steps * rows
    count = group * sr
    shape = (count, rows * local)
    row_id, col_id = iota(shape, 0), iota(shape, 1)
    request, col_request = row_id % rows, col_id // local
    fresh_shape = (count, steps * rows * kv_heads)
    fresh_row, fresh_col = iota(fresh_shape, 0), iota(fresh_shape, 1)
    fresh = (
        (fresh_row % rows == (fresh_col // kv_heads) % rows)
        & (fresh_col // (kv_heads * rows) <= (fresh_row // rows) % steps)
        & (tensor_here == 0)
    )
    fresh_head = jnp.where(fresh, fresh_col % kv_heads, -1)
    lane = iota((sr, LANES), 1)
    per_tile = out_ref.shape[2] // head - 1
    field = LANES // 2 // per_tile
    factor = head ** (-0.5) * LOG2_E
    contract = (((1,), (1,)), ((), ()))
    for copy in copies + cache_copies:
        copy.wait()
    length = jnp.zeros(shape, jnp.int32)
    for r in range(rows):
        length = jnp.where(col_request == r, lengths_ref[r], length)
    visible = (request == col_request) & (tensor_here * local + col_id % local < length)
    for s in range(steps):
        q_rows[s * rows : (s + 1) * rows, :] = q_ref[s].astype(f32)
    new_all = new_ref[...].astype(f32).reshape(steps * rows * kv_heads, 2 * head).astype(bf16)
    new_keys, new_values = new_all[:, :head], new_all[:, head:]
    ones = jnp.ones((rows * local + new_keys.shape[0], head), bf16)
    out_copies = []
    for g in range(kv_heads):
        q = jnp.concatenate(
            [q_rows[:, (g * group + k) * head : (g * group + k + 1) * head] for k in range(group)],
            axis=0,
        ).astype(bf16)
        keys = cache_ref[g, :, :, :head].reshape(rows * local, head)
        values = cache_ref[g, :, :, head:].reshape(rows * local, head)
        keys = jnp.concatenate([keys, new_keys], axis=0)
        values = jnp.concatenate([values, new_values], axis=0)
        values = jnp.concatenate([values, ones], axis=1)
        scores = lax.dot_general(q, keys, contract, preferred_element_type=f32) * factor
        old_scores = jnp.where(visible, scores[:, : rows * local], NEG_LARGE)
        new_scores = jnp.where(fresh_head == g, scores[:, rows * local :], NEG_LARGE)
        top = jnp.max(jnp.maximum(old_scores, new_scores), axis=1, keepdims=True)
        shift = jnp.maximum(top, 0.01 * NEG_LARGE).astype(bf16).astype(f32)
        weights = jnp.concatenate(
            [jnp.exp2(old_scores - shift), jnp.exp2(new_scores - shift)], axis=1
        ).astype(bf16)
        sums = jnp.dot(weights, values, preferred_element_type=f32)
        accum, total = sums[:, :head], sums[:, head:]
        for first in range(0, group, per_tile):
            place = (g * group + first) // per_tile
            stats = jnp.zeros((sr, LANES), f32)
            for k in range(per_tile):
                part = slice((first + k) * sr, (first + k + 1) * sr)
                out_ref[place, :, k * head : (k + 1) * head] = accum[part].astype(bf16)
                stats = jnp.where(lane // field == k, shift[part], stats)
                stats = jnp.where(lane // field == per_tile + k, total[part], stats)
            out_ref[place, :, per_tile * head :] = stats.astype(bf16)
        places = group // per_tile
        here = pl.ds(g * places, places)
        out_copies.append(
            pltpu.make_async_copy(out_ref.at[here], out_hbm.at[here], sent.at[g])
        )
        out_copies[-1].start()
    for copy in plan_copies:
        copy.wait()
    replica_here = lax.axis_index("replica")
    row = iota((steps * rows, LANES), 0) % rows
    page = jnp.zeros((steps * rows, LANES), f32)
    for r in range(rows):
        slot = slots_ref[r]
        entry = jnp.clip(slot - SLOTS, 0, source_slot_ref.shape[0] - 1)
        number = jnp.where(
            slot < SLOTS,
            replica_here * SLOTS + slot,
            source_ref[entry] * SLOTS + source_slot_ref[entry],
        )
        page = jnp.where(row == r, number.astype(f32), page)
    page_ref[...] = page.astype(bf16)
    for copy in out_copies:
        copy.wait()


def send_all(ref, hbm, sent):
    copies = [
        pltpu.make_async_copy(ref, hbm.at[i], sent.at[i]) for i in range(hbm.shape[0])
    ]
    for copy in copies:
        copy.start()
    for copy in copies:
        copy.wait()


def combine_kernel(page_ref, part_ref, attended_ref, send_hbm, send_ref, sent):
    steps, rows, width = attended_ref.shape
    sources = part_ref.shape[0]
    per_tile = width // LANES
    field = LANES // 2 // per_tile
    sr = steps * rows
    stats = part_ref[:, :, width:].astype(f32)
    top = stats[0]
    for t in range(1, sources):
        top = jnp.maximum(top, stats[t])
    fade = jnp.exp2(stats - top[None]).astype(bf16).reshape(sources * sr, LANES)
    lane, column = iota((LANES, width), 0), iota((LANES, width), 1) // LANES * field
    spread = lax.dot(fade, (lane == column).astype(f32).astype(bf16), preferred_element_type=f32)
    totals = lax.dot(
        part_ref[:, :, width:].reshape(sources * sr, LANES),
        (lane == column + LANES // 2).astype(f32).astype(bf16),
        preferred_element_type=f32,
    )
    sums = jnp.zeros((sr, width), f32)
    total = jnp.zeros((sr, width), f32)
    for t in range(sources):
        part = slice(t * sr, (t + 1) * sr)
        sums = sums + spread[part] * part_ref[t, :, :width].astype(f32)
        total = total + spread[part] * totals[part]
    attended_all = sums / total
    for k in range(per_tile):
        attended = attended_all[:, k * LANES : (k + 1) * LANES]
        for s in range(steps):
            attended_ref[s, :, k * LANES : (k + 1) * LANES] = attended[
                s * rows : (s + 1) * rows
            ].astype(bf16)
        rounded = attended.astype(bf16)
        send_ref[:, k * LANES : (k + 1) * LANES] = rounded
    send_ref[:, width:] = page_ref[...]
    send_all(send_ref, send_hbm, sent)


def page_columns(page, first, rank, width):
    return page[:, :1] == (first + iota((page.shape[0], width), 1) // rank).astype(f32)


def page_blocks(refs, at_once):
    replica_here = lax.axis_index("replica")
    for distance, ref in zip(HELD, refs):
        first = jnp.bitwise_xor(replica_here, distance) * SLOTS
        for p in range(0, ref.shape[0], at_once):
            block = ref[p : p + at_once]
            yield first + p, block.reshape(at_once * block.shape[1], block.shape[2])


def shrink_kernel(rows_ref, *refs):
    members, steps_rows, padded = rows_ref.shape
    page_refs = refs[: len(HELD)]
    turn_refs = refs[len(HELD) : -5]
    out_hbm, place_ref, chosen_ref, out_ref, sent = refs[-5:]
    turn = turn_refs[0][0] if turn_refs else 0
    rank, width = page_refs[0].shape[1:]
    count = members * steps_rows
    rows = ROWS
    steps = steps_rows // rows
    data = rows_ref[...].reshape(count, padded)
    x, page = data[:, :width], data[:, width:].astype(f32)
    distance = jnp.bitwise_xor(page.astype(jnp.int32) // SLOTS, lax.axis_index("replica"))
    held = distance == HELD[0]
    for other in HELD[1:]:
        held = held | (distance == other)
    held = held.astype(f32)
    one, other = iota((count, count), 0), iota((count, count), 1)
    earlier = (
        (other // steps_rows * rows + other % rows < one // steps_rows * rows + one % rows)
        & (other % steps_rows < rows)
    ).astype(f32).astype(bf16)
    order = jnp.dot(earlier, held.astype(bf16), preferred_element_type=f32)
    row = iota((count, LANES), 0)
    lane = iota((count, LANES), 1)
    slots = AT_ONCE * steps
    wanted = turn * AT_ONCE + lane // steps
    place = (
        (held > 0.0)
        & (order == wanted.astype(f32))
        & (row % steps_rows // rows == lane % steps)
        & (lane < slots)
    ).astype(f32).astype(bf16)
    place_ref[...] = place
    at_once = 256 // rank
    accum = jnp.zeros((count, at_once * rank), f32)
    for first, block in page_blocks(page_refs, at_once):
        product = lax.dot_general(x, block, (((1,), (1,)), ((), ())), preferred_element_type=f32)
        accum = accum + jnp.where(page_columns(page, first, rank, at_once * rank), product, 0.0)
    folded = accum[:, :LANES] + accum[:, LANES:]
    folded = (folded + pltpu.roll(folded, rank, 1)).astype(bf16)
    down = (((0,), (0,)), ((), ()))
    both = jnp.concatenate([folded, data[:, width:]], axis=1)
    both = lax.dot_general(place[:, :slots], both, down, preferred_element_type=f32)
    folded, chosen_ref[...] = both[:, :LANES], both[:, LANES:]
    half = slots // 2
    packed = jnp.where(iota((half, LANES), 1) < rank, folded[:half], folded[half:]).astype(bf16)
    out_ref[...] = packed
    send_all(out_ref, out_hbm, sent)


def expand_kernel(part_ref, place_ref, chosen_ref, *refs):
    page_refs, out_ref = refs[:-1], refs[-1]
    members, steps_rows, width = out_ref.shape
    rank = page_refs[0].shape[1]
    slots = chosen_ref.shape[0]
    page = chosen_ref[...]
    packed = part_ref[0].astype(f32)
    for t in range(1, part_ref.shape[0]):
        packed = packed + part_ref[t].astype(f32)
    swapped = pltpu.roll(packed, rank, 1)
    left = iota(packed.shape, 1) < rank
    low = jnp.concatenate(
        [jnp.where(left, packed, swapped), jnp.where(left, swapped, packed)], axis=0
    )
    low = jnp.concatenate([low, low], axis=1).astype(bf16).astype(f32)
    at_once = 256 // rank
    accum = jnp.zeros((slots, width), f32)
    for first, block in page_blocks(page_refs, at_once):
        used = jnp.where(page_columns(page, first, rank, at_once * rank), low, 0.0)
        accum = accum + jnp.dot(used.astype(bf16), block, preferred_element_type=f32)
    result = (accum * ADAPTER_SCALE).astype(bf16)
    spread = jnp.dot(place_ref[:, :slots], result, preferred_element_type=f32).astype(bf16)
    out_ref[...] = spread.reshape(members, steps_rows, width)


def gather_kernel(part_ref, out_ref):
    steps, rows, _ = out_ref.shape
    total = part_ref[0].astype(f32)
    for z in range(1, part_ref.shape[0]):
        total = total + part_ref[z].astype(f32)
    for s in range(steps):
        out_ref[s] = total[s * rows : (s + 1) * rows].astype(bf16)


def per_device(
    queries, new_entries, cache, lengths, adapter_pages, request_slots, source_replica, source_slot
):
    replicas, tensors = lax.axis_size("replica"), lax.axis_size("tensor")
    z_size = replicas // X_SIZE
    groups = [
        [z * X_SIZE + (x ^ (z % 2 * X_SIZE // 2)) for z in range(z_size)] for x in range(X_SIZE)
    ]
    members = len(groups[0])
    steps, rows, model = queries.shape
    width = model // tensors
    kv_heads = cache.shape[1]
    rank = adapter_pages.shape[2]
    sr = steps * rows
    count = members * sr

    def exchange(array, distance):
        return lax.ppermute(array, "replica", [(i, i ^ distance) for i in range(replicas)])

    shrink_own, expand_own = adapter_pages[:, 0], adapter_pages[:, 1]
    shrink_pages = [shrink_own] + [exchange(shrink_own, d) for d in HELD[1:]]
    expand_pages = [expand_own] + [in_vmem(exchange(expand_own, d)) for d in HELD[1:]]

    plan = (request_slots, source_replica[:, 0], source_slot)
    parts, page = pl.pallas_call(
        attention_kernel,
        out_shape=(
            pltpu.HBM((tensors, sr, width + LANES), bf16),
            pltpu.VMEM((sr, LANES), bf16),
        ),
        in_specs=[hbm_spec()] * 7,
        out_specs=(hbm_spec(), vmem_spec()),
        scratch_shapes=[
            pltpu.SMEM(lengths.shape, lengths.dtype),
            *[pltpu.SMEM(array.shape, array.dtype) for array in plan],
            pltpu.VMEM(queries.shape, bf16),
            pltpu.VMEM(new_entries.shape, bf16),
            pltpu.VMEM((kv_heads,) + cache.shape[:1] + cache.shape[2:], bf16),
            pltpu.VMEM((sr, model), f32),
            pltpu.VMEM((tensors, sr, width + LANES), bf16),
            pltpu.SemaphoreType.DMA((3 + kv_heads,)),
            pltpu.SemaphoreType.DMA((kv_heads,)),
            pltpu.SemaphoreType.DMA((3,)),
        ],
        compiler_params=params(),
        name="attention_part",
    )(*[in_hbm(array) for array in (lengths, queries, new_entries, cache) + plan])
    parts = lax.all_to_all(parts, "tensor", 0, 0, tiled=True)

    attended, outgoing = pl.pallas_call(
        combine_kernel,
        out_shape=(
            jax.ShapeDtypeStruct((steps, rows, width), bf16),
            pltpu.HBM((members, sr, width + LANES), bf16),
        ),
        in_specs=[vmem_spec(), vmem_spec()],
        out_specs=(vmem_spec(), hbm_spec()),
        scratch_shapes=[
            pltpu.VMEM((sr, width + LANES), bf16),
            pltpu.SemaphoreType.DMA((members,)),
        ],
        compiler_params=params(),
        name="combine",
    )(page, parts)
    column = lax.all_to_all(
        outgoing, "replica", 0, 0, tiled=True, axis_index_groups=groups
    )

    slots = AT_ONCE * steps

    def turn(k):
        number = () if k is None else (jnp.full((1,), k, jnp.int32),)
        low, place, chosen = pl.pallas_call(
            shrink_kernel,
            out_shape=(
                pltpu.HBM((tensors, slots // 2, LANES), bf16),
                jax.ShapeDtypeStruct((count, LANES), bf16),
                jax.ShapeDtypeStruct((slots, LANES), f32),
            ),
            in_specs=[vmem_spec()] * (1 + len(HELD)) + [smem_spec()] * len(number),
            out_specs=(hbm_spec(), vmem_spec(), vmem_spec()),
            scratch_shapes=[
                pltpu.VMEM((slots // 2, LANES), bf16),
                pltpu.SemaphoreType.DMA((tensors,)),
            ],
            compiler_params=params(),
            name="shrink_part",
        )(column, *shrink_pages, *number)
        low = lax.all_to_all(low, "tensor", 0, 0, tiled=True)
        back = pl.pallas_call(
            expand_kernel,
            out_shape=pltpu.VMEM((members, sr, width), bf16),
            in_specs=[vmem_spec()] * (3 + len(HELD)),
            out_specs=vmem_spec(),
            compiler_params=params(),
            name="expand_rows",
        )(low, place, chosen, *expand_pages)
        return back

    back = turn(None)
    distance = (column[:, :rows, width].astype(f32).astype(jnp.int32) // SLOTS) ^ lax.axis_index(
        "replica"
    )
    held = sum(jnp.sum((distance == other).astype(jnp.int32)) for other in HELD)
    _, back = lax.while_loop(
        lambda state: state[0] * AT_ONCE < held,
        lambda state: (state[0] + 1, state[1] + turn(state[0])),
        (jnp.int32(1), back),
    )
    back = lax.all_to_all(back, "replica", 0, 0, tiled=True, axis_index_groups=groups)

    adapted = pl.pallas_call(
        gather_kernel,
        out_shape=jax.ShapeDtypeStruct((steps, rows, width), bf16),
        in_specs=[vmem_spec()],
        out_specs=vmem_spec(),
        compiler_params=params(),
        name="returned_rows",
    )(back)
    return attended, adapted


def solution(mesh):
    return jax.shard_map(
        per_device,
        mesh=mesh,
        in_specs=(
            P(None, "replica", None),
            P(None, "replica", None, None),
            P("replica", None, "tensor", None),
            P("replica"),
            P("replica", None, None, "tensor"),
            P("replica"),
            P("replica", None),
            P("replica"),
        ),
        out_specs=(P(None, "replica", "tensor"), P(None, "replica", "tensor")),
        check_vma=False,
    )
```
